128 devices in a mesh: group: 8 (over y, x_lo), replica: 16 (over x_hi, z, core).
Axes of the slice: x: 4 (x_hi: 2, x_lo: 2; x = x_hi * 2 + x_lo), y: 4, z: 4, core: 2. Of those that a mesh axis runs over, the one named last changes fastest.
Arguments:
- hidden_in: bfloat16 [16, 1024, 896], P('replica', 'group'), may hold values from -6 to 6
- segment_ids: int32 [16, 1024], P('replica'), may hold values from 0 to 2, as said below
- attn_gain: bfloat16 [1, 896], P(None, 'group'), may hold values from 0.5 to 1.5
- w_query: bfloat16 [1, 896, 896], P(None, 'group'), may hold values from -0.1875 to 0.1875
- b_query: bfloat16 [1, 896], P(None, 'group'), may hold values from -3 to 3
- w_key: bfloat16 [1, 896, 128], P(None, 'group'), may hold values from -0.1875 to 0.1875
- b_key: bfloat16 [1, 128], P(None, 'group'), may hold values from -3 to 3
- w_value: bfloat16 [1, 896, 128], P(None, 'group'), may hold values from -0.1875 to 0.1875
- b_value: bfloat16 [1, 128], P(None, 'group'), may hold values from -3 to 3
- w_out: bfloat16 [1, 896, 896], P(None, 'group'), may hold values from -1.5 to 1.5
- ffn_gain: bfloat16 [1, 896], P(None, 'group'), may hold values from 0.5 to 1.5
- w_gate: bfloat16 [1, 896, 4864], P(None, 'group'), may hold values from -0.1875 to 0.1875
- w_up: bfloat16 [1, 896, 4864], P(None, 'group'), may hold values from -0.1875 to 0.1875
- w_down: bfloat16 [1, 4864, 896], P(None, 'group'), may hold values from -0.078125 to 0.078125
- cotangent: bfloat16 [16, 1024, 896], P('replica', 'group'), may hold values from -6 to 6
Outputs:
- hidden_out: bfloat16 [16, 1024, 896], P('replica', 'group')
- grad_in: float32 [16, 1024, 896], P('replica', 'group')
- grad_attn_gain: float32 [1, 896], P(None, 'group')
- grad_w_query: float32 [1, 896, 896], P(None, 'group')
- grad_b_query: float32 [1, 896], P(None, 'group')
- grad_w_key: float32 [1, 896, 128], P(None, 'group')
- grad_b_key: float32 [1, 128], P(None, 'group')
- grad_w_value: float32 [1, 896, 128], P(None, 'group')
- grad_b_value: float32 [1, 128], P(None, 'group')
- grad_w_out: float32 [1, 896, 896], P(None, 'group')
- grad_ffn_gain: float32 [1, 896], P(None, 'group')
- grad_w_gate: float32 [1, 896, 4864], P(None, 'group')
- grad_w_up: float32 [1, 896, 4864], P(None, 'group')
- grad_w_down: float32 [1, 4864, 896], P(None, 'group')
The draws below stay inside these ranges and needn't reach their ends.
Inputs may be any that keep to these rules, and one draw needn't show every extreme that they name: `segment_ids`: each sequence's ids start at 0, never fall and rise by one at each document boundary; a sequence holds one to three documents, each of 204 tokens or more.
All inputs are finite; a program needn't handle non-finite values.
Results may differ from the reference program's by a relative error of at most 0.035.
Values may be sent and summed in bfloat16 or wider, within the bound.
No kernel may reach another device: no remote copies, remote signals or barrier semaphores. Data moves between devices by JAX's collectives and lax.ppermute only.
A program may use at most 128 MiB of HBM per device.

```python
import jax
import jax.numpy as jnp
from jax import lax

D = 896
HEADS = 14
KV_HEADS = 2
HEAD_DIM = 64
FF = 4864
LAYERS = 1
LEN = 1024
HQ = 896
KVW = 128
NSEQ = 16


def draw_segment_ids(key, part):
    key = jax.random.fold_in(key, 11)
    subkeys = jax.random.split(key, 5)
    doc_count = jax.random.randint(subkeys[0], (NSEQ,), 1, 4)
    whole_seq = jax.random.randint(subkeys[1], (), 0, NSEQ)
    three_seq = (whole_seq + jax.random.randint(subkeys[2], (), 1, NSEQ)) % NSEQ
    seq_index = jnp.arange(NSEQ, dtype=jnp.int32)
    doc_count = jnp.where(seq_index == whole_seq, 1, doc_count)
    doc_count = jnp.where(seq_index == three_seq, 3, doc_count)
    first_cut = jax.random.randint(subkeys[3], (NSEQ,), LEN // 5, 2 * LEN // 5)
    second_cut = jax.random.randint(subkeys[4], (NSEQ,), 3 * LEN // 5, 4 * LEN // 5)
    positions = jnp.arange(LEN, dtype=jnp.int32)[None, :]
    first_part = (positions >= first_cut[:, None]).astype(jnp.int32) * (doc_count[:, None] >= 2).astype(jnp.int32)
    second_part = (positions >= second_cut[:, None]).astype(jnp.int32) * (doc_count[:, None] >= 3).astype(jnp.int32)
    return (first_part + second_part).astype(jnp.int32)


def shard_levels(stream_key, extent, pieces, least, high):
    loudness = 1.0
    for axis_at, shards_of in pieces:
        steps = jax.random.uniform(jax.random.fold_in(jax.random.fold_in(stream_key, 6), axis_at), (shards_of,), jnp.float32, least / len(pieces), high / len(pieces))
        loudness = loudness * jnp.repeat(jnp.exp(steps), extent[axis_at] // shards_of).reshape((-1,) + (1,) * (len(extent) - 1 - axis_at))
    return loudness


def bell_draw(own_key, shape, spread, limit, cuts=(), kind=jnp.bfloat16):
    factor_of = shard_levels(own_key, shape, cuts, -0.22, 0.18) if cuts else 1.0
    values = jax.random.normal(own_key, shape, jnp.float32) * spread * factor_of
    return jnp.minimum(jnp.maximum(values, -limit), limit).astype(kind)


def setup_inputs(seed: int = 0) -> dict:
    keys = jax.random.split(jax.random.key(seed), 16)
    return {
        "hidden_in": bell_draw(keys[0], (NSEQ, LEN, D), 1.0, 6.0, ((0, 16), (1, 8))),
        "segment_ids": draw_segment_ids(jax.random.fold_in(keys[15], 71), 0),
        "attn_gain": jnp.clip(1.0 + 0.1 * jax.random.normal(keys[2], (LAYERS, D), jnp.float32), 0.5, 1.5).astype(jnp.bfloat16),
        "w_query": bell_draw(keys[3], (LAYERS, D, HQ), D ** -0.5, 0.1875, ((1, 8),)),
        "b_query": bell_draw(keys[4], (LAYERS, HQ), 0.5, 3.0, ((1, 8),)),
        "w_key": bell_draw(keys[5], (LAYERS, D, KVW), D ** -0.5, 0.1875, ((1, 8),)),
        "b_key": bell_draw(keys[6], (LAYERS, KVW), 0.5, 3.0, ((1, 8),)),
        "w_value": bell_draw(keys[7], (LAYERS, D, KVW), D ** -0.5, 0.1875, ((1, 8),)),
        "b_value": bell_draw(keys[8], (LAYERS, KVW), 0.5, 3.0, ((1, 8),)),
        "w_out": bell_draw(keys[9], (LAYERS, HQ, D), (max(HQ // 64, 1)) ** -0.5, 1.5, ((1, 8),)),
        "ffn_gain": jnp.clip(1.0 + 0.1 * jax.random.normal(keys[10], (LAYERS, D), jnp.float32), 0.5, 1.5).astype(jnp.bfloat16),
        "w_gate": bell_draw(keys[11], (LAYERS, D, FF), D ** -0.5, 0.1875, ((1, 8),)),
        "w_up": bell_draw(keys[12], (LAYERS, D, FF), D ** -0.5, 0.1875, ((1, 8),)),
        "w_down": bell_draw(keys[13], (LAYERS, FF, D), FF ** -0.5, 0.078125, ((1, 8),)),
        "cotangent": bell_draw(keys[14], (NSEQ, LEN, D), 1.0, 6.0, ((0, 16), (1, 8))),
    }


EPS = 1e-06
THETA = 1000000.0
HIGH = lax.Precision.HIGHEST

@jax.custom_vjp
def low(v):
    return lax.optimization_barrier(v.astype(jnp.bfloat16)).astype(jnp.float32)

@jax.custom_vjp
def low_back(v):
    return v

def low_keep(v):
    return (low(v), None)

def low_pass(kept, grad):
    return (grad,)

def back_keep(v):
    return (v, None)

def back_low(kept, grad):
    return (low(grad),)
low.defvjp(low_keep, low_pass)
low_back.defvjp(back_keep, back_low)

def turn_half(values_in):
    half_size = values_in.shape[-1] // 2
    return jnp.concatenate([-values_in[..., half_size:], values_in[..., :half_size]], axis=-1)

def rotate(values_in, cosine_table, sine_table):
    return values_in * cosine_table + turn_half(values_in) * sine_table

def rope_tables(segments):
    positions = jnp.arange(LEN, dtype=jnp.int32)[None, :] - lax.optimization_barrier(jnp.sum((segments[:, None, :] < segments[:, :, None]).astype(jnp.int32), axis=-1))
    half_size = HEAD_DIM // 2
    frequency = THETA ** (-(2.0 * jnp.arange(half_size, dtype=jnp.float32)) / HEAD_DIM)
    angles = positions.reshape(-1).astype(jnp.float32)[:, None] * frequency
    cosine_table = jnp.concatenate([jnp.cos(angles), jnp.cos(angles)], axis=-1)[:, None, :]
    sine_table = jnp.concatenate([jnp.sin(angles), jnp.sin(angles)], axis=-1)[:, None, :]
    return (cosine_table, sine_table)

def product(left_side, right_side):
    return jnp.dot(left_side, right_side, precision=HIGH, preferred_element_type=jnp.float32)

def rms_norm(stream, gain_vector):
    return stream * lax.rsqrt(lax.optimization_barrier(jnp.mean(stream * stream, axis=-1, keepdims=True)) + EPS) * gain_vector

def attend(packed):
    queries, keys_in, values_in, segments = packed
    ratio = HEADS // KV_HEADS
    query_heads = queries.reshape(LEN, KV_HEADS, ratio, HEAD_DIM)
    key_heads = keys_in.reshape(LEN, KV_HEADS, HEAD_DIM)
    value_heads = values_in.reshape(LEN, KV_HEADS, HEAD_DIM)
    raw_scores = low_back(jnp.einsum('qcgd,kcd->cgqk', query_heads, key_heads, precision=HIGH))
    indices = jnp.arange(LEN, dtype=jnp.int32)
    allowed = (indices[None, :] <= indices[:, None]) & (segments[None, :] == segments[:, None])
    scores = jnp.where(allowed, raw_scores * HEAD_DIM ** (-0.5), -1e+30)
    probs = low(jax.nn.softmax(scores, axis=-1))
    mixed = jnp.einsum('cgqk,kcd->qcgd', probs, value_heads, precision=HIGH)
    return mixed.reshape(LEN, HEADS * HEAD_DIM)

def forward(stream, parameters, cosine_table, sine_table, segments):
    first_gain, query_weight, query_bias, key_weight, key_bias, value_weight, value_bias, out_weight, second_gain, gate_weight, up_weight, down_weight = parameters
    token_rows = stream.shape[0]
    for layer_index in range(LAYERS):
        normed = low(rms_norm(stream, first_gain[layer_index]))
        raw_query = low_back(product(normed, query_weight[layer_index]) + query_bias[layer_index])
        raw_key = low_back(product(normed, key_weight[layer_index]) + key_bias[layer_index])
        raw_value = low_back(product(normed, value_weight[layer_index]) + value_bias[layer_index])
        queries = low(rotate(raw_query.reshape(token_rows, HEADS, HEAD_DIM), cosine_table, sine_table))
        keys_all = low(rotate(raw_key.reshape(token_rows, KV_HEADS, HEAD_DIM), cosine_table, sine_table))
        values_all = low(raw_value)
        mixed = lax.map(jax.checkpoint(attend), (queries.reshape(NSEQ, LEN, -1), keys_all.reshape(NSEQ, LEN, -1), values_all.reshape(NSEQ, LEN, -1), segments))
        attended = low(low_back(mixed.reshape(token_rows, -1)))
        stream = stream + low_back(product(attended, out_weight[layer_index]))
        second_normed = low(rms_norm(stream, second_gain[layer_index]))
        gate_value = low_back(product(second_normed, gate_weight[layer_index]))
        up_value = low_back(product(second_normed, up_weight[layer_index]))
        hidden = low(jax.nn.silu(gate_value) * up_value)
        stream = stream + low_back(product(hidden, down_weight[layer_index]))
    return stream

def reference(hidden_in, segment_ids, attn_gain, w_query, b_query, w_key, b_key, w_value, b_value, w_out, ffn_gain, w_gate, w_up, w_down, cotangent):
    cosine_table, sine_table = rope_tables(segment_ids)
    parameters = tuple((member.astype(jnp.float32) for member in (attn_gain, w_query, b_query, w_key, b_key, w_value, b_value, w_out, ffn_gain, w_gate, w_up, w_down)))
    start_stream = hidden_in.astype(jnp.float32).reshape(NSEQ * LEN, D)

    def run_layers(stream, *weights):
        return forward(stream, weights, cosine_table, sine_table, segment_ids)
    final_stream, pullback = jax.vjp(run_layers, start_stream, *parameters)
    gradients = pullback(cotangent.astype(jnp.float32).reshape(NSEQ * LEN, D))
    hidden_out = final_stream.reshape(NSEQ, LEN, D).astype(jnp.bfloat16)
    return (hidden_out, gradients[0].reshape(NSEQ, LEN, D), gradients[1], gradients[2], gradients[3], gradients[4], gradients[5], gradients[6], gradients[7], gradients[8], gradients[9], gradients[10], gradients[11], gradients[12])
```

```python
import jax
import jax.numpy as jnp
from jax import lax
from jax.sharding import Mesh
from jax.sharding import PartitionSpec as P

KV_HEADS = 2
HEAD_DIM = 64
EPS = 1e-06
THETA = 1000000.0
MASKED_SCORE = -1e30
GROUP = ("y", "xl")
REPLICA = ("xh", "z", "c")
SIZES = (4, 2, 2, 4, 2)
AXES = ("y", "xl", "xh", "z", "c")
N = 8
PAD = 640
BF = jnp.bfloat16
F32 = jnp.float32


def shift(array, axis, by, size):
    return lax.ppermute(array, axis, [(i, (i + by) % size) for i in range(size)])


def gather_slots(array):
    return [array] + [shift(array, GROUP, -k, N) for k in range(1, N)]


def return_slots(slots):
    total = slots[0].astype(F32)
    for k in range(1, N):
        total = total + shift(slots[k], GROUP, k, N).astype(F32)
    return total


def at(blocks, index):
    return lax.dynamic_index_in_dim(blocks, index, 0, keepdims=False)


def to_all(array):
    return lax.all_to_all(jnp.broadcast_to(array, (N, *array.shape)), GROUP, 0, 0, tiled=True)


def turn_half(values_in):
    half_size = values_in.shape[-1] // 2
    return jnp.concatenate([-values_in[..., half_size:], values_in[..., :half_size]], axis=-1)


def rotate(values_in, cosine_table, sine_table):
    return values_in * cosine_table + turn_half(values_in) * sine_table


def rotate_back(gradient, cosine_table, sine_table):
    return gradient * cosine_table - turn_half(gradient * sine_table)


def norm_forward(stream, gain):
    scale = lax.rsqrt(jnp.mean(stream * stream, axis=-1, keepdims=True) + EPS)
    return stream * scale * gain, scale


def norm_backward(stream, scale, gain, gradient):
    normalized = stream * scale
    scaled = gradient * gain
    gain_grad = jnp.sum(gradient * normalized, axis=0)
    grad = scale * (scaled - normalized * jnp.mean(scaled * normalized, axis=-1, keepdims=True))
    return grad, gain_grad


def mm(a, b):
    return jnp.dot(a, b, preferred_element_type=F32)


def mm_t(a, b):
    return lax.dot_general(a, b, (((1,), (1,)), ((), ())), preferred_element_type=F32)


def outer(a, b):
    return lax.dot_general(a, b, (((0,), (0,)), ((), ())), preferred_element_type=F32)


def core_sum(first, second, c):
    low = c == 0
    keep = jnp.where(low, first, second)
    send = jnp.where(low, second, first).astype(BF)
    return (keep + shift(send, "c", 1, 2).astype(F32)).astype(BF)


def core_pair(own, c):
    other = shift(own, "c", 1, 2)
    low = c == 0
    return jnp.where(low, own, other), jnp.where(low, other, own)


def spread_sum(blocks, z, xh):
    total = at(blocks, z).astype(F32)
    for k in (1, 3, 2):
        total = total + shift(at(blocks, (z + k) % 4), "z", k, 4).astype(F32)
    send = at(total, 1 - xh).astype(BF)
    return (at(total, xh) + shift(send, "xh", 1, 2).astype(F32)).astype(BF)


def spread_gather(piece, z, xh):
    other = shift(piece, "xh", 1, 2)
    low = xh == 0
    pair = jnp.stack([jnp.where(low, piece, other), jnp.where(low, other, piece)])
    slots = jnp.stack([pair] + [shift(pair, "z", -k, 4) for k in (1, 2, 3)])
    return [at(slots, (j // 2 - z) % 4)[j % 2] for j in range(8)]


def swap_pairs():
    pairs = []
    for y in range(4):
        for xl in range(2):
            for xh in range(2):
                for z in range(4):
                    for c in range(2):
                        source = (((y * 2 + xl) * 2 + xh) * 4 + z) * 2 + c
                        target = (((z * 2 + xh) * 2 + xl) * 4 + y) * 2 + c
                        pairs.append((source, target))
    return pairs


def local(
    hidden_in,
    segment_ids,
    attn_gain,
    w_query,
    b_query,
    w_key,
    b_key,
    w_value,
    b_value,
    w_out,
    ffn_gain,
    w_gate,
    w_up,
    w_down,
    cotangent,
):
    g = lax.axis_index(GROUP)
    c = lax.axis_index("c")
    z = lax.axis_index("z")
    xh = lax.axis_index("xh")
    rows, width = hidden_in.shape[1:]
    part = w_query.shape[1]
    units = w_down.shape[1]
    kv = w_key.shape[2]
    heads = width // HEAD_DIM
    ratio = heads // KV_HEADS

    segments = segment_ids[0]
    length = segments.shape[0]
    own_segments = lax.dynamic_slice_in_dim(segments, g * rows, rows, 0)
    query_index = g * rows + jnp.arange(rows, dtype=jnp.int32)
    earlier = jnp.sum((segments[None, :] < own_segments[:, None]).astype(jnp.int32), axis=-1)
    positions = query_index - earlier
    blocks = (g - jnp.arange(N, dtype=jnp.int32)) % N
    key_index = (blocks[:, None] * rows + jnp.arange(rows, dtype=jnp.int32)[None]).reshape(-1)
    doubled = jnp.concatenate([segments.reshape(N, rows)] * 2, axis=0)
    key_segments = lax.dynamic_slice_in_dim(doubled, g + 1, N, 0)[::-1].reshape(-1)
    allowed = (key_index[None, :] <= query_index[:, None]) & (
        key_segments[None, :] == own_segments[:, None]
    )
    half = HEAD_DIM // 2
    frequency = THETA ** (-(2.0 * jnp.arange(half, dtype=F32)) / HEAD_DIM)
    angles = positions.astype(F32)[:, None] * frequency
    cosine = jnp.concatenate([jnp.cos(angles)] * 2, axis=-1)[:, None, :]
    sine = jnp.concatenate([jnp.sin(angles)] * 2, axis=-1)[:, None, :]

    small = jnp.concatenate([attn_gain[0], b_query[0], b_key[0], b_value[0], ffn_gain[0]])
    small = jnp.pad(small[None], ((0, 15), (0, width + 2 * kv - small.shape[0])))
    packed = jnp.concatenate(
        [jnp.concatenate([w_query[0], w_key[0], w_value[0]], axis=1), small], axis=0
    )
    fetched = to_all(packed)
    w_qkv = fetched[:, :part].reshape(width, width + 2 * kv)
    vec = fetched[:, part].astype(F32)
    k16 = kv // N
    first_gain = vec[:, :part].reshape(-1)
    bias = jnp.concatenate(
        [
            vec[:, part : 2 * part].reshape(-1),
            vec[:, 2 * part : 2 * part + k16].reshape(-1),
            vec[:, 2 * part + k16 : 2 * part + 2 * k16].reshape(-1),
        ]
    )
    second_gain = vec[:, 2 * part + 2 * k16 : 3 * part + 2 * k16].reshape(-1)
    out_weight = to_all(w_out[0]).reshape(width, width)

    def pad_units(w):
        return jnp.pad(w.reshape(part, N, units), ((0, 0), (0, 0), (0, PAD - units)))

    gate_up = jnp.moveaxis(jnp.concatenate([pad_units(w_gate[0]), pad_units(w_up[0])], -1), 1, 0)
    w_gu = lax.all_to_all(gate_up, GROUP, 0, 0, tiled=True).reshape(width, 2 * PAD)
    w_dn = jnp.pad(w_down[0], ((0, PAD - units), (0, 0)))
    group_down = jnp.concatenate(gather_slots(cotangent[0]))

    stream = hidden_in[0].astype(F32)
    normed, first_scale = norm_forward(stream, first_gain)
    normed = normed.astype(BF)
    raw = mm(normed, w_qkv) + bias
    turned = rotate(raw[:, : width + kv].reshape(rows, -1, HEAD_DIM), cosine, sine)
    turned = turned.reshape(rows, -1).astype(BF)
    queries = turned[:, :width].reshape(rows, KV_HEADS, ratio, HEAD_DIM)
    own_kv = jnp.concatenate([turned[:, width:], raw[:, width + kv :].astype(BF)], axis=1)
    slots = [own_kv]
    for k in range(1, N):
        slots.append(lax.ppermute(own_kv, GROUP, [(i, i + k) for i in range(N - k)]))
    all_kv = jnp.concatenate(slots)
    keys = all_kv[:, :kv].reshape(length, KV_HEADS, HEAD_DIM)
    values = all_kv[:, kv:].reshape(length, KV_HEADS, HEAD_DIM)
    scores = jnp.einsum("qcgd,kcd->cgqk", queries, keys, preferred_element_type=F32)
    scores = jnp.where(allowed[None, None], scores * HEAD_DIM ** (-0.5), MASKED_SCORE)
    maximum = jnp.max(scores, axis=-1, keepdims=True)
    weights = jnp.exp(scores - maximum)
    totals = jnp.sum(weights, axis=-1, keepdims=True)
    probs = (weights / totals).astype(BF)
    mixed = jnp.einsum("cgqk,kcd->qcgd", probs, values, preferred_element_type=F32)
    attended = mixed.reshape(rows, -1).astype(BF)
    logsum = maximum + jnp.log(totals)
    middle = stream + mm(attended, out_weight)

    second_normed, second_scale = norm_forward(middle, second_gain)
    group_second = jnp.concatenate(gather_slots(second_normed.astype(BF)))
    both = mm(group_second, w_gu)
    gate, up = both[:, :PAD], both[:, PAD:]
    sigmoid = jax.nn.sigmoid(gate)
    hidden = (gate * sigmoid * up).astype(BF)
    grad_hidden = mm_t(group_down, w_dn)
    grad_gate = (grad_hidden * up * sigmoid * (1.0 + gate * (1.0 - sigmoid))).astype(BF)
    grad_up = (grad_hidden * gate * sigmoid).astype(BF)
    grad_both = jnp.concatenate([grad_gate, grad_up], axis=1)
    second_terms = mm_t(grad_both, w_gu).astype(BF)
    grad_second = return_slots([second_terms[k * rows : (k + 1) * rows] for k in range(N)])
    down_terms = mm(hidden, w_dn).astype(BF)
    layer_out = middle + return_slots([down_terms[k * rows : (k + 1) * rows] for k in range(N)])
    hidden_out = layer_out.astype(BF)[None]

    shares = core_sum(outer(group_second, grad_gate), outer(group_second, grad_up), c)
    share = spread_sum(shares.reshape(4, 2, part, PAD), z, xh)
    share = lax.ppermute(share, AXES, swap_pairs())
    columns = jnp.stack(spread_gather(share, z, xh))
    columns = core_pair(columns, c)

    def unpad(array):
        return jnp.moveaxis(array[:, :, :units], 0, 1).reshape(1, part, N * units).astype(F32)

    grad_w_gate, grad_w_up = unpad(columns[0]), unpad(columns[1])
    down_share = outer(hidden, group_down)
    half_rows = PAD // 2
    down_share = core_sum(down_share[:half_rows], down_share[half_rows:], c)
    down_share = spread_sum(down_share.reshape(4, 2, PAD // 16, width), z, xh)
    down_share = jnp.concatenate(spread_gather(down_share, z, xh))
    grad_w_down = jnp.concatenate(core_pair(down_share, c))[None, :units].astype(F32)

    stream_grad = cotangent[0].astype(F32)
    term, gain_second = norm_backward(middle, second_scale, second_gain, grad_second)
    grad_middle = stream_grad + term
    attn_grad = grad_middle.astype(BF)
    grad_attended = mm_t(attn_grad, out_weight).astype(BF)
    grad_out = outer(attended, attn_grad)
    grad_split = grad_attended.reshape(queries.shape)
    probs = jnp.exp(scores - logsum)
    grad_probs = jnp.einsum("qcgd,kcd->cgqk", grad_split, values, preferred_element_type=F32)
    inner = jnp.sum(probs * grad_probs, axis=-1, keepdims=True)
    grad_scores = (probs * (grad_probs - inner) * HEAD_DIM ** (-0.5)).astype(BF)
    grad_queries = jnp.einsum("cgqk,kcd->qcgd", grad_scores, keys, preferred_element_type=F32)
    grad_keys = jnp.einsum("cgqk,qcgd->kcd", grad_scores, queries, preferred_element_type=F32)
    grad_values = jnp.einsum(
        "cgqk,qcgd->kcd", probs.astype(BF), grad_split, preferred_element_type=F32
    )
    grad_kv = jnp.concatenate([grad_keys.reshape(length, kv), grad_values.reshape(length, kv)], 1)
    own = grad_kv[:rows]
    grad_kv = grad_kv.astype(BF)
    for k in range(1, N):
        block = grad_kv[k * rows : (k + 1) * rows]
        own = own + lax.ppermute(block, GROUP, [(i, i - k) for i in range(k, N)]).astype(F32)
    grad_qk = jnp.concatenate([grad_queries.reshape(rows, width), own[:, :kv]], axis=1)
    grad_qk = rotate_back(grad_qk.reshape(rows, -1, HEAD_DIM), cosine, sine).reshape(rows, -1)
    grad_qkv = jnp.concatenate([grad_qk, own[:, kv:]], axis=1).astype(BF)
    grad_first = mm_t(grad_qkv, w_qkv)
    term, gain_first = norm_backward(stream, first_scale, first_gain, grad_first)
    grad_in = (grad_middle + term)[None]

    outer_qkv = outer(normed, grad_qkv)
    bias_grad = jnp.sum(grad_qkv.astype(F32), axis=0)
    lanes = width + kv
    row_a = jnp.concatenate(
        [
            bias_grad[:width].reshape(N, part),
            bias_grad[width : width + kv].reshape(N, k16),
            bias_grad[width + kv :].reshape(N, k16),
        ],
        axis=1,
    )
    row_b = jnp.concatenate([gain_first.reshape(N, part), gain_second.reshape(N, part)], axis=1)

    def with_row(array, row):
        row = jnp.pad(row[:, None], ((0, 0), (0, 15), (0, lanes - row.shape[1])))
        return jnp.concatenate([array.reshape(N, part, lanes), row], axis=1)

    side_a = with_row(outer_qkv[:, :lanes], row_a)
    side_b = with_row(jnp.concatenate([grad_out, outer_qkv[:, lanes:]], axis=1), row_b)
    shares = core_sum(side_a, side_b, c)
    total = at(shares, g).astype(F32)
    for k in range(1, N):
        total = total + shift(at(shares, (g + k) % N), GROUP, k, N).astype(F32)
    pieces = jnp.moveaxis(total.astype(BF).reshape(part + 16, 4, 2, lanes // 8), 0, 2)
    piece = spread_sum(pieces, z, xh)
    whole = jnp.concatenate(spread_gather(piece, z, xh), axis=1)
    whole_a, whole_b = [half_side.astype(F32) for half_side in core_pair(whole, c)]
    last_a, last_b = whole_a[part], whole_b[part]
    return (
        hidden_out,
        grad_in,
        last_b[None, :part],
        whole_a[None, :part, :width],
        last_a[None, :part],
        whole_a[None, :part, width:],
        last_a[None, part : part + k16],
        whole_b[None, :part, width:],
        last_a[None, part + k16 : part + 2 * k16],
        whole_b[None, :part, :width],
        last_b[None, part : 2 * part],
        grad_w_gate,
        grad_w_up,
        grad_w_down,
    )


def solution(mesh):
    split = Mesh(mesh.devices.reshape(SIZES), AXES)
    tokens = P(REPLICA, GROUP, None)
    vector = P(None, GROUP)
    matrix = P(None, GROUP, None)
    weights = (vector, matrix, vector, matrix, vector, matrix, vector, matrix, vector)
    return jax.shard_map(
        local,
        mesh=split,
        in_specs=(tokens, P(REPLICA, None)) + weights + (matrix,) * 3 + (tokens,),
        out_specs=(tokens, tokens) + weights + (matrix,) * 3,
        check_vma=False,
    )
```

```python
import jax
import jax.numpy as jnp
from jax import lax
from jax.experimental import pallas as pl
from jax.experimental.pallas import tpu as pltpu
from jax.sharding import Mesh
from jax.sharding import PartitionSpec as P

KV_HEADS = 2
HEAD_DIM = 64
EPS = 1e-06
THETA = 1000000.0
MASKED_SCORE = -1e30
GROUP = ("y", "xl")
SPREAD = ("z", "xh")
REPLICA = ("xh", "z", "c")
SIZES = (4, 2, 2, 4, 2)
AXES = ("y", "xl", "xh", "z", "c")
N = 8
PAD = 640
HALF = 64
BF = jnp.bfloat16
F32 = jnp.float32


def shift(array, axis, by, size):
    return lax.ppermute(array, axis, [(i, (i + by) % size) for i in range(size)])


def exchange(blocks, axis):
    return lax.all_to_all(blocks, axis, 0, 0, tiled=True)


def to_all(array, axis):
    return exchange(jnp.broadcast_to(array, (N, *array.shape)), axis)


def sum_at(blocks, axis):
    return jnp.sum(exchange(blocks, axis).astype(F32), axis=0)


def at(blocks, index):
    return lax.dynamic_index_in_dim(blocks, index, 0, keepdims=False)


def turn_half(values_in):
    half_size = values_in.shape[-1] // 2
    return jnp.concatenate([-values_in[..., half_size:], values_in[..., :half_size]], axis=-1)


def rotate(values_in, cosine_table, sine_table):
    return values_in * cosine_table + turn_half(values_in) * sine_table


def rotate_back(gradient, cosine_table, sine_table):
    return gradient * cosine_table - turn_half(gradient * sine_table)


def norm_forward(stream, gain):
    scale = lax.rsqrt(jnp.mean(stream * stream, axis=-1, keepdims=True) + EPS)
    return stream * scale * gain, scale


def norm_backward(stream, scale, gain, gradient):
    normalized = stream * scale
    scaled = gradient * gain
    gain_grad = jnp.sum(gradient * normalized, axis=0)
    grad = scale * (scaled - normalized * jnp.mean(scaled * normalized, axis=-1, keepdims=True))
    return grad, gain_grad


def mm(a, b):
    return jnp.dot(a, b, preferred_element_type=F32)


def mm_t(a, b):
    return lax.dot_general(a, b, (((1,), (1,)), ((), ())), preferred_element_type=F32)


def outer(a, b):
    return lax.dot_general(a, b, (((0,), (0,)), ((), ())), preferred_element_type=F32)


def core_sum(first, second, c):
    low = c == 0
    keep = jnp.where(low, first, second)
    send = jnp.where(low, second, first).astype(BF)
    return (keep + shift(send, "c", 1, 2).astype(F32)).astype(BF)


def core_pair(own, c):
    other = shift(own, "c", 1, 2)
    low = c == 0
    return jnp.where(low, own, other), jnp.where(low, other, own)


def pack_units(w_ref, packed_ref):
    units = w_ref.shape[1] // N
    packed_ref[...] = jnp.zeros_like(packed_ref)
    for j in range(N):
        packed_ref[j, :, :units] = w_ref[:, j * units : (j + 1) * units]


def unpack_units(core_ref, own_ref, other_ref, gate_ref, up_ref):
    units = gate_ref.shape[1] // N

    def write(source, target):
        for j in range(N):
            target[:, j * units : (j + 1) * units] = source[j, :, :units].astype(F32)

    @pl.when(core_ref[0] == 0)
    def _():
        write(own_ref, gate_ref)
        write(other_ref, up_ref)

    @pl.when(core_ref[0] != 0)
    def _():
        write(other_ref, gate_ref)
        write(own_ref, up_ref)


VMEM = pl.BlockSpec(memory_space=pltpu.VMEM)
SMEM = pl.BlockSpec(memory_space=pltpu.SMEM)


def call(kernel, outs, *args, specs=None, mib=32):
    return pl.pallas_call(
        kernel,
        out_shape=outs,
        in_specs=specs or [VMEM] * len(args),
        out_specs=jax.tree.map(lambda _: VMEM, outs),
        compiler_params=pltpu.CompilerParams(vmem_limit_bytes=mib * 2**20),
    )(*args)


def swap_pairs():
    pairs = []
    for y in range(4):
        for xl in range(2):
            for xh in range(2):
                for z in range(4):
                    for c in range(2):
                        source = (((y * 2 + xl) * 2 + xh) * 4 + z) * 2 + c
                        target = (((z * 2 + xh) * 2 + xl) * 4 + y) * 2 + c
                        pairs.append((source, target))
    return pairs


def local(
    hidden_in,
    segment_ids,
    attn_gain,
    w_query,
    b_query,
    w_key,
    b_key,
    w_value,
    b_value,
    w_out,
    ffn_gain,
    w_gate,
    w_up,
    w_down,
    cotangent,
):
    g = lax.axis_index(GROUP)
    c = lax.axis_index("c")
    rows, width = hidden_in.shape[1:]
    part = w_query.shape[1]
    units = w_down.shape[1]
    kv = w_key.shape[2]
    heads = width // HEAD_DIM
    ratio = heads // KV_HEADS

    segments = segment_ids[0]
    length = segments.shape[0]
    own_segments = lax.dynamic_slice_in_dim(segments, g * rows, rows, 0)
    query_index = g * rows + jnp.arange(rows, dtype=jnp.int32)
    earlier = jnp.sum((segments[None, :] < own_segments[:, None]).astype(jnp.int32), axis=-1)
    positions = query_index - earlier
    key_index = jnp.arange(length, dtype=jnp.int32)
    allowed = (key_index[None, :] <= query_index[:, None]) & (
        segments[None, :] == own_segments[:, None]
    )
    half = HEAD_DIM // 2
    frequency = THETA ** (-(2.0 * jnp.arange(half, dtype=F32)) / HEAD_DIM)
    angles = positions.astype(F32)[:, None] * frequency
    cosine = jnp.concatenate([jnp.cos(angles)] * 2, axis=-1)[:, None, :]
    sine = jnp.concatenate([jnp.sin(angles)] * 2, axis=-1)[:, None, :]

    small = jnp.concatenate([attn_gain[0], b_query[0], b_key[0], b_value[0], ffn_gain[0]])
    small = jnp.pad(small[None], ((0, 15), (0, width + 2 * kv - small.shape[0])))
    packed = jnp.concatenate(
        [jnp.concatenate([w_query[0], w_key[0], w_value[0]], axis=1), small], axis=0
    )
    halves = packed.reshape(2, HALF, width + 2 * kv)
    fetched = jnp.concatenate(core_pair(to_all(at(halves, c), GROUP), c), axis=1)
    w_qkv = fetched[:, :part].reshape(width, width + 2 * kv)
    vec = fetched[:, part].astype(F32)
    k16 = kv // N
    first_gain = vec[:, :part].reshape(-1)
    bias = jnp.concatenate(
        [
            vec[:, part : 2 * part].reshape(-1),
            vec[:, 2 * part : 2 * part + k16].reshape(-1),
            vec[:, 2 * part + k16 : 2 * part + 2 * k16].reshape(-1),
        ]
    )
    second_gain = vec[:, 2 * part + 2 * k16 : 3 * part + 2 * k16].reshape(-1)
    out_weight = lax.all_gather(w_out[0], GROUP, axis=0, tiled=True)
    group_down = lax.all_gather(cotangent[0], GROUP, axis=0, tiled=True)
    mine = jnp.where(c == 0, w_gate[0], w_up[0])
    mine = call(pack_units, jax.ShapeDtypeStruct((N, part, PAD), BF), mine)
    pair = core_pair(exchange(mine, GROUP), c)
    w_gu = jnp.concatenate([half_side.reshape(width, PAD) for half_side in pair], axis=1)
    w_dn = jnp.pad(w_down[0], ((0, PAD - units), (0, 0)))

    stream = hidden_in[0].astype(F32)
    normed, first_scale = norm_forward(stream, first_gain)
    normed = normed.astype(BF)
    raw = mm(normed, w_qkv) + bias
    turned = rotate(raw[:, : width + kv].reshape(rows, -1, HEAD_DIM), cosine, sine)
    turned = turned.reshape(rows, -1).astype(BF)
    queries = turned[:, :width].reshape(rows, KV_HEADS, ratio, HEAD_DIM)
    own_kv = jnp.concatenate([turned[:, width:], raw[:, width + kv :].astype(BF)], axis=1)
    all_kv = to_all(own_kv, GROUP).reshape(length, 2 * kv)
    keys = all_kv[:, :kv].reshape(length, KV_HEADS, HEAD_DIM)
    values = all_kv[:, kv:].reshape(length, KV_HEADS, HEAD_DIM)
    scores = jnp.einsum("qcgd,kcd->cgqk", queries, keys, preferred_element_type=F32)
    scores = jnp.where(allowed[None, None], scores * HEAD_DIM ** (-0.5), MASKED_SCORE)
    maximum = jnp.max(scores, axis=-1, keepdims=True)
    weights = jnp.exp(scores - maximum)
    totals = jnp.sum(weights, axis=-1, keepdims=True)
    probs = (weights / totals).astype(BF)
    mixed = jnp.einsum("cgqk,kcd->qcgd", probs, values, preferred_element_type=F32)
    attended = mixed.reshape(rows, -1).astype(BF)
    logsum = maximum + jnp.log(totals)
    middle = stream + mm(attended, out_weight)

    second_normed, second_scale = norm_forward(middle, second_gain)
    group_second = to_all(second_normed.astype(BF), GROUP).reshape(length, width)
    both = mm(group_second, w_gu)
    gate, up = both[:, :PAD], both[:, PAD:]
    sigmoid = jax.nn.sigmoid(gate)
    hidden = (gate * sigmoid * up).astype(BF)
    grad_hidden = mm_t(group_down, w_dn)
    grad_gate = (grad_hidden * up * sigmoid * (1.0 + gate * (1.0 - sigmoid))).astype(BF)
    grad_up = (grad_hidden * gate * sigmoid).astype(BF)
    grad_both = jnp.concatenate([grad_gate, grad_up], axis=1)
    second_terms = mm_t(grad_both, w_gu).astype(BF)
    grad_second = sum_at(second_terms.reshape(N, rows, width), GROUP)
    down_terms = mm(hidden, w_dn).astype(BF)
    grad_second, down_terms = lax.optimization_barrier((grad_second, down_terms))
    layer_out = middle + sum_at(down_terms.reshape(N, rows, width), GROUP)
    hidden_out = layer_out.astype(BF)[None]

    shares = core_sum(outer(group_second, grad_gate), outer(group_second, grad_up), c)
    share = sum_at(shares.reshape(N, part, PAD), SPREAD).astype(BF)
    share = lax.ppermute(share, AXES, swap_pairs())
    columns = to_all(share, SPREAD)
    other = shift(columns, "c", 1, 2)
    grads = (jax.ShapeDtypeStruct((part, N * units), F32),) * 2
    unpacked = call(unpack_units, grads, c.reshape(1), columns, other, specs=[SMEM, VMEM, VMEM])
    grad_w_gate, grad_w_up = unpacked[0][None], unpacked[1][None]
    down_share = outer(hidden, group_down)
    down_rows = PAD // 2
    down_share = core_sum(down_share[:down_rows], down_share[down_rows:], c)

    stream_grad = cotangent[0].astype(F32)
    term, gain_second = norm_backward(middle, second_scale, second_gain, grad_second)
    grad_middle = stream_grad + term
    attn_grad = grad_middle.astype(BF)
    grad_attended = mm_t(attn_grad, out_weight).astype(BF)
    small = jnp.pad(gain_second.reshape(N, 1, part), ((0, 0), (0, 15), (0, width - part)))
    grad_out = outer(attended, attn_grad).reshape(N, part, width)
    grad_out = jnp.concatenate([grad_out, small], axis=1)
    out_share = sum_at(core_sum(grad_out[:, :HALF], grad_out[:, HALF:], c), GROUP).astype(BF)
    share = jnp.concatenate([down_share, out_share]).reshape(N, -1, width)
    share = to_all(sum_at(share, SPREAD).astype(BF), SPREAD).reshape(-1, width)
    low, high = core_pair(share, c)
    grad_w_down = jnp.concatenate([low[:down_rows], high[:down_rows]])[None, :units].astype(F32)
    grad_out = jnp.concatenate([low[down_rows:], high[down_rows:]]).astype(F32)
    grad_split = grad_attended.reshape(queries.shape)
    probs = jnp.exp(scores - logsum)
    grad_probs = jnp.einsum("qcgd,kcd->cgqk", grad_split, values, preferred_element_type=F32)
    inner = jnp.sum(probs * grad_probs, axis=-1, keepdims=True)
    grad_scores = (probs * (grad_probs - inner) * HEAD_DIM ** (-0.5)).astype(BF)
    grad_queries = jnp.einsum("cgqk,kcd->qcgd", grad_scores, keys, preferred_element_type=F32)
    grad_keys = jnp.einsum("cgqk,qcgd->kcd", grad_scores, queries, preferred_element_type=F32)
    grad_values = jnp.einsum(
        "cgqk,qcgd->kcd", probs.astype(BF), grad_split, preferred_element_type=F32
    )
    grad_kv = jnp.concatenate([grad_keys.reshape(length, kv), grad_values.reshape(length, kv)], 1)
    own = sum_at(grad_kv.astype(BF).reshape(N, rows, 2 * kv), GROUP)
    grad_qk = jnp.concatenate([grad_queries.reshape(rows, width), own[:, :kv]], axis=1)
    grad_qk = rotate_back(grad_qk.reshape(rows, -1, HEAD_DIM), cosine, sine).reshape(rows, -1)
    grad_qkv = jnp.concatenate([grad_qk, own[:, kv:]], axis=1).astype(BF)
    grad_first = mm_t(grad_qkv, w_qkv)
    term, gain_first = norm_backward(stream, first_scale, first_gain, grad_first)
    grad_in = (grad_middle + term)[None]

    outer_qkv = outer(normed, grad_qkv)
    bias_grad = jnp.sum(grad_qkv.astype(F32), axis=0)
    row = jnp.concatenate(
        [
            bias_grad[:width].reshape(N, part),
            bias_grad[width : width + kv].reshape(N, k16),
            bias_grad[width + kv :].reshape(N, k16),
            gain_first.reshape(N, part),
        ],
        axis=1,
    )
    row = jnp.pad(row[:, None], ((0, 0), (0, 15), (0, width + 2 * kv - row.shape[1])))
    share = jnp.concatenate([outer_qkv.reshape(N, part, -1), row], axis=1)
    share = sum_at(core_sum(share[:, :HALF], share[:, HALF:], c), GROUP).astype(BF)
    share = sum_at(share.reshape(N, HALF // N, -1), SPREAD).astype(BF)
    share = to_all(share, SPREAD).reshape(HALF, -1)
    whole = jnp.concatenate(core_pair(share, c)).astype(F32)
    last = whole[part]
    return (
        hidden_out,
        grad_in,
        last[None, part + 2 * k16 : 2 * part + 2 * k16],
        whole[None, :part, :width],
        last[None, :part],
        whole[None, :part, width : width + kv],
        last[None, part : part + k16],
        whole[None, :part, width + kv :],
        last[None, part + k16 : part + 2 * k16],
        grad_out[None, :part],
        grad_out[part, :part][None],
        grad_w_gate,
        grad_w_up,
        grad_w_down,
    )


def solution(mesh):
    split = Mesh(mesh.devices.reshape(SIZES), AXES)
    tokens = P(REPLICA, GROUP, None)
    vector = P(None, GROUP)
    matrix = P(None, GROUP, None)
    weights = (vector, matrix, vector, matrix, vector, matrix, vector, matrix, vector)
    return jax.shard_map(
        local,
        mesh=split,
        in_specs=(tokens, P(REPLICA, None)) + weights + (matrix,) * 3 + (tokens,),
        out_specs=(tokens, tokens) + weights + (matrix,) * 3,
        check_vma=False,
    )
```

```python
import jax
import jax.numpy as jnp
from jax import lax
from jax.experimental import pallas as pl
from jax.experimental.pallas import tpu as pltpu
from jax.sharding import Mesh
from jax.sharding import PartitionSpec as P

KV_HEADS = 2
HEAD_DIM = 64
EPS = 1e-06
THETA = 1000000.0
MASKED_SCORE = -1e30
GROUP = ("y", "xl")
SPREAD = ("z", "xh")
REPLICA = ("xh", "z", "c")
SIZES = (4, 2, 2, 4, 2)
AXES = ("y", "xl", "xh", "z", "c")
N = 8
PAD = 640
HALF = 64
BF = jnp.bfloat16
F32 = jnp.float32


def shift(array, axis, by, size):
    return lax.ppermute(array, axis, [(i, (i + by) % size) for i in range(size)])


def exchange(blocks, axis):
    return lax.all_to_all(blocks, axis, 0, 0, tiled=True)


def to_all(array, axis):
    return exchange(jnp.broadcast_to(array, (N, *array.shape)), axis)


def sum_at(blocks, axis):
    return jnp.sum(exchange(blocks, axis).astype(F32), axis=0)


def at(blocks, index):
    return lax.dynamic_index_in_dim(blocks, index, 0, keepdims=False)


def norm_forward(stream, gain):
    scale = lax.rsqrt(jnp.mean(stream * stream, axis=-1, keepdims=True) + EPS)
    return stream * scale * gain, scale


def norm_backward(stream, scale, gain, gradient):
    normalized = stream * scale
    scaled = gradient * gain
    gain_grad = jnp.sum(gradient * normalized, axis=0)
    grad = scale * (scaled - normalized * jnp.mean(scaled * normalized, axis=-1, keepdims=True))
    return grad, gain_grad


def mm(a, b):
    return jnp.dot(a, b, preferred_element_type=F32)


def mm_t(a, b):
    return lax.dot_general(a, b, (((1,), (1,)), ((), ())), preferred_element_type=F32)


def outer(a, b):
    return lax.dot_general(a, b, (((0,), (0,)), ((), ())), preferred_element_type=F32)


def core_sum(first, second, c):
    low = c == 0
    keep = jnp.where(low, first, second)
    send = jnp.where(low, second, first).astype(BF)
    return (keep + shift(send, "c", 1, 2).astype(F32)).astype(BF)


def core_pair(own, c):
    other = shift(own, "c", 1, 2)
    low = c == 0
    return jnp.where(low, own, other), jnp.where(low, other, own)


def pack_units(w_ref, packed_ref):
    units = w_ref.shape[1] // N
    packed_ref[...] = jnp.zeros_like(packed_ref)
    for j in range(N):
        packed_ref[j, :, :units] = w_ref[:, j * units : (j + 1) * units]


def unpack_units(blocks_ref, gate_ref, up_ref):
    units = gate_ref.shape[1] // N
    for i, target in enumerate((gate_ref, up_ref)):
        for j in range(N):
            target[:, j * units : (j + 1) * units] = blocks_ref[j, i, :, :units].astype(F32)


VMEM = pl.BlockSpec(memory_space=pltpu.VMEM)
SMEM = pl.BlockSpec(memory_space=pltpu.SMEM)


def call(kernel, outs, *args, scalars=0, scratch=(), flops=0, mib=48):
    cost = pl.CostEstimate(flops=flops, bytes_accessed=2**20, transcendentals=0)
    return pl.pallas_call(
        kernel,
        out_shape=outs,
        in_specs=[SMEM] * scalars + [VMEM] * (len(args) - scalars),
        out_specs=jax.tree.map(lambda _: VMEM, outs),
        scratch_shapes=[pltpu.VMEM(shape, dtype) for shape, dtype in scratch],
        compiler_params=pltpu.CompilerParams(vmem_limit_bytes=mib * 2**20),
        cost_estimate=cost,
    )(*args)


def pack_weights(core_ref, q_ref, k_ref, v_ref, row_ref, out_ref):
    part = q_ref.shape[0]
    width, kv = q_ref.shape[1], k_ref.shape[1]
    spans = ((0, q_ref), (width, k_ref), (width + kv, v_ref))

    @pl.when(core_ref[0] == 0)
    def _():
        for j in range(N):
            for start, ref in spans:
                out_ref[j, :, start : start + ref.shape[1]] = ref[:HALF]

    @pl.when(core_ref[0] != 0)
    def _():
        for j in range(N):
            for start, ref in spans:
                out_ref[j, : part - HALF, start : start + ref.shape[1]] = ref[HALF:]
            out_ref[j, part - HALF :] = row_ref[...]


def dot(a, b, da, db):
    return lax.dot_general(a, b, (((da,), (db,)), ((), ())), preferred_element_type=F32)


def turned_rows(block, cos, sin, back):
    half = HEAD_DIM // 2
    top, low = block[:half], block[half:]
    if back:
        return [top * cos + low * sin, low * cos - top * sin]
    return [top * cos - low * sin, low * cos + top * sin]


def project_tokens(core_ref, x_ref, own_ref, other_ref, cos_ref, sin_ref, w_ref, rows_ref, q_ref, kv_ref, n_ref, scale_ref):
    part = w_ref.shape[0] // N
    width = x_ref.shape[1]
    lanes = w_ref.shape[1]
    kv = (lanes - width) // 2

    def assemble(low, high):
        small = jnp.zeros((16, lanes), F32)
        for j in range(N):
            w_ref[part * j : part * j + HALF] = low[j]
            w_ref[part * j + HALF : part * (j + 1)] = high[j, : part - HALF]
            small = small + high[j, part - HALF :].astype(F32)
        rows_ref[...] = small

    @pl.when(core_ref[0] == 0)
    def _():
        assemble(own_ref, other_ref)

    @pl.when(core_ref[0] != 0)
    def _():
        assemble(other_ref, own_ref)

    x = x_ref[...].astype(F32)
    scale = lax.rsqrt(jnp.mean(x * x, axis=-1, keepdims=True) + EPS)
    scale_ref[...] = scale
    normed = (x * scale * rows_ref[0:1, :width]).astype(BF)
    n_ref[...] = normed
    raw = dot(normed, w_ref[...], 1, 0) + rows_ref[1:2, :]
    kv_ref[:, kv:] = raw[:, width + kv :].astype(BF)
    turned = raw[:, : width + kv].T
    cos, sin = cos_ref[...], sin_ref[...]
    for h in range(width // HEAD_DIM):
        block = turned[h * HEAD_DIM : (h + 1) * HEAD_DIM]
        q_ref[h * HEAD_DIM : (h + 1) * HEAD_DIM] = jnp.concatenate(
            turned_rows(block, cos, sin, False)
        ).astype(BF)
    keys = []
    for h in range(width // HEAD_DIM, (width + kv) // HEAD_DIM):
        keys += turned_rows(turned[h * HEAD_DIM : (h + 1) * HEAD_DIM], cos, sin, False)
    kv_ref[:, :kv] = jnp.concatenate(keys).T.astype(BF)


CHUNK = 256


def heads_side_by_side(ref, first, ratio):
    return jnp.concatenate(
        [ref[(first + i) * HEAD_DIM : (first + i + 1) * HEAD_DIM] for i in range(ratio)], axis=1
    )


def mask_bias(start, group, key_ref, own_ref, rows, ratio):
    key = start + lax.broadcasted_iota(jnp.int32, (CHUNK, rows), 0)
    query = group * rows + lax.broadcasted_iota(jnp.int32, (CHUNK, rows), 1)
    allowed = (key <= query) & (key_ref[start : start + CHUNK] == own_ref[...])
    bias = jnp.where(allowed, 0.0, MASKED_SCORE)
    return jnp.concatenate([bias] * ratio, axis=1)


def attend_kernel(group_ref, q_ref, kv_ref, key_ref, own_ref, out_ref, log_ref, score_ref):
    rows = q_ref.shape[1]
    length = kv_ref.shape[0]
    kv = kv_ref.shape[1] // 2
    ratio = q_ref.shape[0] // kv
    starts = range(0, length, CHUNK)
    for head in range(KV_HEADS):
        queries = heads_side_by_side(q_ref, head * ratio, ratio) * BF(HEAD_DIM**-0.5)
        span = slice(head * HEAD_DIM, (head + 1) * HEAD_DIM)
        top = jnp.full((1, ratio * rows), MASKED_SCORE, F32)
        for start in starts:
            scores = dot(kv_ref[start : start + CHUNK, span], queries, 1, 0)
            scores = scores + mask_bias(start, group_ref[0], key_ref, own_ref, rows, ratio)
            score_ref[start : start + CHUNK] = scores
            top = jnp.maximum(top, jnp.max(scores, axis=0, keepdims=True))
        total = jnp.zeros_like(top)
        mixed = jnp.zeros((HEAD_DIM, ratio * rows), F32)
        for start in starts:
            weights = jnp.exp(score_ref[start : start + CHUNK] - top)
            total = total + jnp.sum(weights, axis=0, keepdims=True)
            values = kv_ref[start : start + CHUNK, kv:][:, span]
            mixed = mixed + dot(values, weights.astype(BF), 0, 0)
        log_ref[head : head + 1] = top + jnp.log(total)
        mixed = (mixed / total).astype(BF)
        for i in range(ratio):
            at_head = (head * ratio + i) * HEAD_DIM
            out_ref[at_head : at_head + HEAD_DIM] = mixed[:, i * rows : (i + 1) * rows]


def attend_back_kernel(group_ref, q_ref, kv_ref, key_ref, own_ref, grad_ref, log_ref, cos_ref, sin_ref, gq_ref, gkv_ref, prob_ref, diff_ref):
    rows = q_ref.shape[1]
    length = kv_ref.shape[0]
    kv = kv_ref.shape[1] // 2
    ratio = q_ref.shape[0] // kv
    starts = range(0, length, CHUNK)
    cos, sin = cos_ref[...], sin_ref[...]
    grads_k, grads_v = [[], []], [[], []]
    for head in range(KV_HEADS):
        queries = heads_side_by_side(q_ref, head * ratio, ratio) * BF(HEAD_DIM**-0.5)
        grads = heads_side_by_side(grad_ref, head * ratio, ratio)
        span = slice(head * HEAD_DIM, (head + 1) * HEAD_DIM)
        log = log_ref[head : head + 1]
        inner = jnp.zeros((1, ratio * rows), F32)
        for start in starts:
            scores = dot(kv_ref[start : start + CHUNK, span], queries, 1, 0)
            scores = scores + mask_bias(start, group_ref[0], key_ref, own_ref, rows, ratio)
            probs = jnp.exp(scores - log)
            prob_ref[start : start + CHUNK] = probs
            diff = dot(kv_ref[start : start + CHUNK, kv:][:, span], grads, 1, 0)
            diff_ref[start : start + CHUNK] = diff
            inner = inner + jnp.sum(probs * diff, axis=0, keepdims=True)
        grad_q = jnp.zeros((HEAD_DIM, ratio * rows), F32)
        for start in starts:
            probs = prob_ref[start : start + CHUNK]
            grad_s = (probs * (diff_ref[start : start + CHUNK] - inner)).astype(BF)
            grads_k[head].append(dot(grad_s, queries, 1, 1))
            grads_v[head].append(dot(probs.astype(BF), grads, 1, 1))
            grad_q = grad_q + dot(kv_ref[start : start + CHUNK, span], grad_s, 0, 0)
        grad_q = grad_q * HEAD_DIM**-0.5
        blocks = []
        for i in range(ratio):
            blocks += turned_rows(grad_q[:, i * rows : (i + 1) * rows], cos, sin, True)
        lanes = ratio * HEAD_DIM
        gq_ref[:, head * lanes : (head + 1) * lanes] = jnp.concatenate(blocks).T.astype(BF)
    for i, start in enumerate(starts):
        parts = [grads_k[0][i], grads_k[1][i], grads_v[0][i], grads_v[1][i]]
        gkv_ref[start : start + CHUNK] = jnp.concatenate(parts, axis=1).astype(BF)


def tail_kernel(core_ref, arrived_ref, gq_ref, w_ref, x_ref, scale_ref, rows_ref, n_ref, mid_ref, cos_ref, sin_ref, in_ref, keep_ref, send_ref, g_ref, share_ref):
    rows, width = x_ref.shape
    lanes = w_ref.shape[1]
    kv = (lanes - width) // 2
    part = width // N
    total = arrived_ref[0].astype(F32)
    for j in range(1, N):
        total = total + arrived_ref[j].astype(F32)
    turned = total[:, :kv].T
    keys = []
    for h in range(KV_HEADS):
        block = turned[h * HEAD_DIM : (h + 1) * HEAD_DIM]
        keys += turned_rows(block, cos_ref[...], sin_ref[...], True)
    g_ref[:, :width] = gq_ref[...]
    g_ref[:, width : width + kv] = jnp.concatenate(keys).T.astype(BF)
    g_ref[:, width + kv :] = total[:, kv:].astype(BF)
    grads = g_ref[...]
    first = dot(grads, w_ref[...], 1, 1)
    scale = scale_ref[...]
    normalized = x_ref[...].astype(F32) * scale
    scaled = first * rows_ref[0:1, :width]
    mean = jnp.mean(scaled * normalized, axis=-1, keepdims=True)
    in_ref[...] = mid_ref[...] + scale * (scaled - normalized * mean)
    gain = jnp.sum(first * normalized, axis=0, keepdims=True)
    share_ref[...] = dot(n_ref[...], grads, 0, 0)
    bias = jnp.sum(grads.astype(F32), axis=0, keepdims=True)
    gain = jnp.concatenate([gain, jnp.zeros((1, lanes - width), F32)], axis=1)
    small = jnp.concatenate([bias, gain, jnp.zeros((14, lanes), F32)])

    def write(low, high):
        for j in range(N):
            low[j] = share_ref[part * j : part * j + HALF].astype(low.dtype)
            high[j, : part - HALF] = share_ref[part * j + HALF : part * (j + 1)].astype(high.dtype)
            high[j, part - HALF :] = small.astype(high.dtype)

    @pl.when(core_ref[0] == 0)
    def _():
        write(keep_ref, send_ref)

    @pl.when(core_ref[0] != 0)
    def _():
        write(send_ref, keep_ref)


def swap_pairs():
    pairs = []
    for group in range(N):
        for spread in range(N):
            for c in range(2):
                pairs.append(((group * N + spread) * 2 + c, (spread * N + group) * 2 + c))
    return pairs


def shape(dtype, *dims):
    return jax.ShapeDtypeStruct(dims, dtype)


def local(
    hidden_in,
    segment_ids,
    attn_gain,
    w_query,
    b_query,
    w_key,
    b_key,
    w_value,
    b_value,
    w_out,
    ffn_gain,
    w_gate,
    w_up,
    w_down,
    cotangent,
):
    g = lax.axis_index(GROUP)
    c = lax.axis_index("c")
    rows, width = hidden_in.shape[1:]
    part = w_query.shape[1]
    units = w_down.shape[1]
    kv = w_key.shape[2]
    heads = width // HEAD_DIM

    lanes = width + 2 * kv
    k16 = kv // N
    core, group = c.reshape(1), g.reshape(1)

    def spread_out(vector):
        place = jnp.arange(N * vector.shape[0]) // vector.shape[0] == g
        return jnp.where(place, jnp.tile(vector, N), BF(0))

    bias = [spread_out(b[0]) for b in (b_query, b_key, b_value)]
    blank = jnp.zeros((2 * kv,), BF)
    small = jnp.stack(
        [
            jnp.concatenate([spread_out(attn_gain[0]), blank]),
            jnp.concatenate(bias),
            jnp.concatenate([spread_out(ffn_gain[0]), blank]),
        ]
    )
    small = jnp.pad(small, ((0, 13), (0, 0)))
    halves = call(
        pack_weights, shape(BF, N, HALF, lanes), core, w_query[0], w_key[0], w_value[0], small, scalars=1
    )
    own_half = exchange(halves, GROUP)
    own_half, w_gate, w_up, w_out, cotangent = lax.optimization_barrier(
        (own_half, w_gate, w_up, w_out, cotangent)
    )
    other_half = shift(own_half, "c", 1, 2)

    segments = segment_ids[0]
    length = segments.shape[0]
    own_segments = lax.dynamic_slice_in_dim(segments, g * rows, rows, 0)
    query_index = g * rows + jnp.arange(rows, dtype=jnp.int32)
    earlier = jnp.sum((segments[None, :] < own_segments[:, None]).astype(jnp.int32), axis=-1)
    positions = query_index - earlier
    half = HEAD_DIM // 2
    frequency = THETA ** (-(2.0 * jnp.arange(half, dtype=F32)) / HEAD_DIM)
    angles = positions.astype(F32)[None, :] * frequency[:, None]
    cosine, sine = jnp.cos(angles), jnp.sin(angles)
    key_segments, own_segments = segments[:, None], own_segments[None]

    w_qkv, gains, queries, own_kv, normed, first_scale = call(
        project_tokens,
        (
            shape(BF, width, lanes),
            shape(F32, 16, lanes),
            shape(BF, width, rows),
            shape(BF, rows, 2 * kv),
            shape(BF, rows, width),
            shape(F32, rows, 1),
        ),
        core,
        hidden_in[0],
        own_half,
        other_half,
        cosine,
        sine,
        scalars=1,
    )
    second_gain = gains[2, :width]
    all_kv = to_all(own_kv, GROUP).reshape(length, 2 * kv)

    mine = jnp.where(c == 0, w_gate[0], w_up[0])
    mine = call(pack_units, shape(BF, N, part, PAD), mine)
    out_weight = lax.all_gather(w_out[0], GROUP, axis=0, tiled=True)
    all_kv, mine, cotangent = lax.optimization_barrier((all_kv, mine, cotangent))
    group_down = lax.all_gather(cotangent[0], GROUP, axis=0, tiled=True)
    pair = core_pair(exchange(mine, GROUP), c)
    w_gu = jnp.concatenate([half_side.reshape(width, PAD) for half_side in pair], axis=1)
    w_dn = jnp.pad(w_down[0], ((0, PAD - units), (0, 0)))

    wide = heads // KV_HEADS * rows
    attended, logsum = call(
        attend_kernel,
        (shape(BF, width, rows), shape(F32, KV_HEADS, wide)),
        group,
        queries,
        all_kv,
        key_segments,
        own_segments,
        scalars=1,
        scratch=[((length, wide), F32)],
    )
    stream = hidden_in[0].astype(F32)
    middle = stream + outer(attended, out_weight)

    second_normed, second_scale = norm_forward(middle, second_gain)
    group_second = to_all(second_normed.astype(BF), GROUP).reshape(length, width)
    both = mm(group_second, w_gu)
    gate, up = both[:, :PAD], both[:, PAD:]
    sigmoid = jax.nn.sigmoid(gate)
    hidden = (gate * sigmoid * up).astype(BF)
    grad_hidden = mm_t(group_down, w_dn)
    grad_gate = (grad_hidden * up * sigmoid * (1.0 + gate * (1.0 - sigmoid))).astype(BF)
    grad_up = (grad_hidden * gate * sigmoid).astype(BF)
    grad_both = jnp.concatenate([grad_gate, grad_up], axis=1)
    second_terms = mm_t(grad_both, w_gu).astype(BF)
    grad_second = sum_at(second_terms.reshape(N, rows, width), GROUP)
    down_terms = mm(hidden, w_dn).astype(BF)
    grad_second, down_terms = lax.optimization_barrier((grad_second, down_terms))
    layer_out = middle + sum_at(down_terms.reshape(N, rows, width), GROUP)
    hidden_out = layer_out.astype(BF)[None]

    shares = [outer(group_second, grad).astype(BF) for grad in (grad_gate, grad_up)]
    shares = jnp.stack([share.reshape(N, part, PAD) for share in shares], axis=1)
    shares = shares.reshape(2 * N * part, PAD)
    share = lax.psum_scatter(shares, REPLICA, scatter_dimension=0, tiled=True)
    share = lax.ppermute(share, AXES, swap_pairs())
    columns = lax.all_gather(share, REPLICA, axis=0, tiled=True).reshape(N, 2, part, PAD)
    grads = (shape(F32, part, N * units),) * 2
    grad_w_gate, grad_w_up = [grad[None] for grad in call(unpack_units, grads, columns)]
    down_share = outer(hidden, group_down)
    down_rows = PAD // 2
    down_share = core_sum(down_share[:down_rows], down_share[down_rows:], c)

    stream_grad = cotangent[0].astype(F32)
    term, gain_second = norm_backward(middle, second_scale, second_gain, grad_second)
    grad_middle = stream_grad + term
    attn_grad = grad_middle.astype(BF)
    grad_attended = mm_t(out_weight, attn_grad).astype(BF)
    small = jnp.pad(gain_second.reshape(N, 1, part), ((0, 0), (0, 15), (0, width - part)))
    grad_out = mm(attended, attn_grad).reshape(N, part, width)
    grad_out = jnp.concatenate([grad_out, small], axis=1)
    out_share = sum_at(core_sum(grad_out[:, :HALF], grad_out[:, HALF:], c), GROUP).astype(BF)
    share = jnp.concatenate([down_share, out_share]).reshape(N, -1, width)
    share = to_all(sum_at(share, SPREAD).astype(BF), SPREAD).reshape(-1, width)
    low, high = core_pair(share, c)
    grad_w_down = jnp.concatenate([low[:down_rows], high[:down_rows]])[None, :units].astype(F32)
    grad_out = jnp.concatenate([low[down_rows:], high[down_rows:]]).astype(F32)
    grad_q, grad_kv = call(
        attend_back_kernel,
        (shape(BF, rows, width), shape(BF, length, 2 * kv)),
        group,
        queries,
        all_kv,
        key_segments,
        own_segments,
        grad_attended,
        logsum,
        cosine,
        sine,
        scalars=1,
        scratch=[((length, wide), F32)] * 2,
    )
    arrived = exchange(grad_kv.reshape(N, rows, 2 * kv), GROUP)

    grad_in, keep, send = call(
        tail_kernel,
        (shape(F32, rows, width), shape(F32, N, HALF, lanes), shape(BF, N, HALF, lanes)),
        core,
        arrived,
        grad_q,
        w_qkv,
        hidden_in[0],
        first_scale,
        gains,
        normed,
        grad_middle,
        cosine,
        sine,
        scalars=1,
        scratch=[((rows, lanes), BF), ((width, lanes), F32)],
    )
    grad_in = grad_in[None]
    share = (keep + shift(send, "c", 1, 2).astype(F32)).astype(BF)
    share = sum_at(share, GROUP).astype(BF)
    share = sum_at(share.reshape(N, HALF // N, -1), SPREAD).astype(BF)
    share = to_all(share, SPREAD).reshape(HALF, -1)
    whole = jnp.concatenate(core_pair(share, c)).astype(F32)
    bias, gain = whole[part], whole[part + 1]

    def own_part(vector, start, size):
        return lax.dynamic_slice_in_dim(vector, start + g * size, size, 0)[None]

    return (
        hidden_out,
        grad_in,
        own_part(gain, 0, part),
        whole[None, :part, :width],
        own_part(bias, 0, part),
        whole[None, :part, width : width + kv],
        own_part(bias, width, k16),
        whole[None, :part, width + kv :],
        own_part(bias, width + kv, k16),
        grad_out[None, :part],
        grad_out[part, :part][None],
        grad_w_gate,
        grad_w_up,
        grad_w_down,
    )


def solution(mesh):
    split = Mesh(mesh.devices.reshape(SIZES), AXES)
    tokens = P(REPLICA, GROUP, None)
    vector = P(None, GROUP)
    matrix = P(None, GROUP, None)
    weights = (vector, matrix, vector, matrix, vector, matrix, vector, matrix, vector)
    return jax.shard_map(
        local,
        mesh=split,
        in_specs=(tokens, P(REPLICA, None)) + weights + (matrix,) * 3 + (tokens,),
        out_specs=(tokens, tokens) + weights + (matrix,) * 3,
        check_vma=False,
    )
```

```python
import functools

import jax
import jax.numpy as jnp
from jax import lax
from jax.experimental import pallas as pl
from jax.experimental.pallas import tpu as pltpu
from jax.sharding import Mesh
from jax.sharding import PartitionSpec as P

KV_HEADS = 2
HEAD_DIM = 64
EPS = 1e-06
THETA = 1000000.0
MASKED_SCORE = -1e30
GROUP = ("y", "xl")
SPREAD = ("xh", "z")
REPLICA = ("xh", "z", "c")
SIZES = (4, 2, 2, 4, 2)
AXES = ("y", "xl", "xh", "z", "c")
N = 8
PAD = 640
HALF = 64
BF = jnp.bfloat16
F32 = jnp.float32


def shift(array, axis, by, size):
    return lax.ppermute(array, axis, [(i, (i + by) % size) for i in range(size)])


def exchange(blocks, axis):
    return lax.all_to_all(blocks, axis, 0, 0, tiled=True)


def to_all(array, axis):
    return exchange(jnp.broadcast_to(array, (N, *array.shape)), axis)


def sum_at(blocks, axis):
    return jnp.sum(exchange(blocks, axis).astype(F32), axis=0)


def at(blocks, index):
    return lax.dynamic_index_in_dim(blocks, index, 0, keepdims=False)


def norm_forward(stream, gain):
    scale = lax.rsqrt(jnp.mean(stream * stream, axis=-1, keepdims=True) + EPS)
    return stream * scale * gain, scale


def norm_backward(stream, scale, gain, gradient):
    normalized = stream * scale
    scaled = gradient * gain
    gain_grad = jnp.sum(gradient * normalized, axis=0)
    grad = scale * (scaled - normalized * jnp.mean(scaled * normalized, axis=-1, keepdims=True))
    return grad, gain_grad


def mm(a, b):
    return jnp.dot(a, b, preferred_element_type=F32)


def mm_t(a, b):
    return lax.dot_general(a, b, (((1,), (1,)), ((), ())), preferred_element_type=F32)


def outer(a, b):
    return lax.dot_general(a, b, (((0,), (0,)), ((), ())), preferred_element_type=F32)


def core_sum(first, second, c):
    low = c == 0
    keep = jnp.where(low, first, second)
    send = jnp.where(low, second, first).astype(BF)
    return (keep + shift(send, "c", 1, 2).astype(F32)).astype(BF)


def core_pair(own, c):
    other = shift(own, "c", 1, 2)
    low = c == 0
    return jnp.where(low, own, other), jnp.where(low, other, own)


def unpack_units(place_ref, own_ref, other_ref, gate_ref, up_ref):
    units = gate_ref.shape[1] // N
    c, z, xh = place_ref[0], place_ref[1], place_ref[2]

    def write(source, target):
        for piece in range(target.shape[0] // 16):
            slot = lax.rem(piece % 4 + 4 - z, 4)
            second = lax.rem(xh + piece // 4, 2)
            for j in range(N):
                for t in range(5):
                    count = min(128, units - 128 * t)
                    row, lane = 16 * (t // 2), 128 * (t % 2)
                    tile = source[slot, second, j, row : row + 16, lane : lane + count]
                    start = units * j + 128 * t
                    target[16 * piece : 16 * piece + 16, start : start + count] = tile.astype(F32)

    @pl.when(c == 0)
    def _():
        write(own_ref, gate_ref)
        write(other_ref, up_ref)

    @pl.when(c != 0)
    def _():
        write(other_ref, gate_ref)
        write(own_ref, up_ref)


VMEM = pl.BlockSpec(memory_space=pltpu.VMEM)
SMEM = pl.BlockSpec(memory_space=pltpu.SMEM)


def call(kernel, outs, *args, scalars=0, scratch=(), flops=0, mib=48):
    cost = pl.CostEstimate(flops=flops, bytes_accessed=2**20, transcendentals=0)
    return pl.pallas_call(
        kernel,
        out_shape=outs,
        in_specs=[SMEM] * scalars + [VMEM] * (len(args) - scalars),
        out_specs=jax.tree.map(lambda _: VMEM, outs),
        scratch_shapes=[pltpu.VMEM(shape, dtype) for shape, dtype in scratch],
        compiler_params=pltpu.CompilerParams(vmem_limit_bytes=mib * 2**20),
        cost_estimate=cost,
    )(*args)


SIDE = 384


def pack_weights(place_ref, q_ref, k_ref, v_ref, row_ref, gate_ref, up_ref, out_ref):
    part = q_ref.shape[0]
    width, kv = q_ref.shape[1], k_ref.shape[1]
    lanes = width + 2 * kv
    units = gate_ref.shape[1] // N
    spans = ((0, q_ref), (width, k_ref), (width + kv, v_ref))
    out_ref[:, :, lanes:] = jnp.zeros((N, HALF, SIDE), BF)
    first = pl.multiple_of(piece_start(place_ref[1], part), 16)

    def beside(ref):
        for j in range(N):
            for t in range(5):
                count = min(128, units - 128 * t)
                start = units * j + 128 * t
                row, lane = 32 * (t // 3), lanes + 128 * (t % 3)
                tile = ref[pl.ds(first, 32), start : start + count]
                out_ref[j, row : row + 32, lane : lane + count] = tile

    @pl.when(place_ref[0] == 0)
    def _():
        beside(gate_ref)
        for j in range(N):
            for start, ref in spans:
                out_ref[j, :, start : start + ref.shape[1]] = ref[:HALF]

    @pl.when(place_ref[0] != 0)
    def _():
        beside(up_ref)
        for j in range(N):
            for start, ref in spans:
                out_ref[j, : part - HALF, start : start + ref.shape[1]] = ref[HALF:]
            out_ref[j, part - HALF :, :lanes] = row_ref[...]


def piece_start(z, part):
    return jnp.minimum(32 * z, part - 32)


def join_units(place_ref, own_ref, other_ref, own_z_ref, other_z_ref, w_ref):
    part = w_ref.shape[0] // N
    lanes = own_ref.shape[2] - SIDE
    z = place_ref[1]

    def write(sources, side):
        near, far = sources

        @pl.loop(0, N)
        def _(j):
            for k in range(4):
                start = part * j + piece_start(lax.rem(z + k, 4), part)
                rows = pl.ds(pl.multiple_of(start, 16), 32)
                for t in range(5):
                    row, lane = 32 * (t // 3), 128 * (t % 3)
                    if k == 0:
                        tile = near[j, row : row + 32, lanes + lane : lanes + lane + 128]
                    else:
                        tile = far[k - 1, j, row : row + 32, lane : lane + 128]
                    column = side * PAD + 128 * t
                    w_ref[rows, column : column + 128] = tile

    @pl.when(place_ref[0] == 0)
    def _():
        write((own_ref, own_z_ref), 0)
        write((other_ref, other_z_ref), 1)

    @pl.when(place_ref[0] != 0)
    def _():
        write((own_ref, own_z_ref), 1)
        write((other_ref, other_z_ref), 0)


def dot(a, b, da, db):
    return lax.dot_general(a, b, (((da,), (db,)), ((), ())), preferred_element_type=F32)


def turned_rows(block, cos, sin, back):
    half = HEAD_DIM // 2
    top, low = block[:half], block[half:]
    if back:
        return [top * cos + low * sin, low * cos - top * sin]
    return [top * cos - low * sin, low * cos + top * sin]


def project_tokens(core_ref, x_ref, own_ref, other_ref, cos_ref, sin_ref, w_ref, rows_ref, q_ref, kv_ref, n_ref, scale_ref):
    part = w_ref.shape[0] // N
    width = x_ref.shape[1]
    lanes = w_ref.shape[1]
    kv = (lanes - width) // 2

    def assemble(low, high):
        small = jnp.zeros((16, lanes), F32)
        for j in range(N):
            w_ref[part * j : part * j + HALF] = low[j, :, :lanes]
            w_ref[part * j + HALF : part * (j + 1)] = high[j, : part - HALF, :lanes]
            small = small + high[j, part - HALF :, :lanes].astype(F32)
        rows_ref[...] = small

    @pl.when(core_ref[0] == 0)
    def _():
        assemble(own_ref, other_ref)

    @pl.when(core_ref[0] != 0)
    def _():
        assemble(other_ref, own_ref)

    x = x_ref[...].astype(F32)
    scale = lax.rsqrt(jnp.mean(x * x, axis=-1, keepdims=True) + EPS)
    scale_ref[...] = scale
    normed = (x * scale * rows_ref[0:1, :width]).astype(BF)
    n_ref[...] = normed
    raw = dot(normed, w_ref[...], 1, 0) + rows_ref[1:2, :]
    kv_ref[:, kv:] = raw[:, width + kv :].astype(BF)
    turned = raw[:, : width + kv].T
    cos, sin = cos_ref[...], sin_ref[...]
    for h in range(width // HEAD_DIM):
        block = turned[h * HEAD_DIM : (h + 1) * HEAD_DIM]
        q_ref[h * HEAD_DIM : (h + 1) * HEAD_DIM] = jnp.concatenate(
            turned_rows(block, cos, sin, False)
        ).astype(BF)
    keys = []
    for h in range(width // HEAD_DIM, (width + kv) // HEAD_DIM):
        keys += turned_rows(turned[h * HEAD_DIM : (h + 1) * HEAD_DIM], cos, sin, False)
    kv_ref[:, :kv] = jnp.concatenate(keys).T.astype(BF)


CHUNK = 256


def heads_side_by_side(ref, first, ratio):
    return jnp.concatenate(
        [ref[(first + i) * HEAD_DIM : (first + i + 1) * HEAD_DIM] for i in range(ratio)], axis=1
    )


def mask_bias(start, group, key_ref, own_ref, rows, ratio):
    key = start + lax.broadcasted_iota(jnp.int32, (CHUNK, rows), 0)
    query = group * rows + lax.broadcasted_iota(jnp.int32, (CHUNK, rows), 1)
    allowed = (key <= query) & (key_ref[start : start + CHUNK] == own_ref[...])
    bias = jnp.where(allowed, 0.0, MASKED_SCORE)
    return jnp.concatenate([bias] * ratio, axis=1)


def attend_kernel(group_ref, q_ref, kv_ref, key_ref, own_ref, out_ref, log_ref, score_ref):
    rows = q_ref.shape[1]
    length = kv_ref.shape[0]
    kv = kv_ref.shape[1] // 2
    ratio = q_ref.shape[0] // kv
    starts = range(0, length, CHUNK)
    for head in range(KV_HEADS):
        queries = heads_side_by_side(q_ref, head * ratio, ratio) * BF(HEAD_DIM**-0.5)
        span = slice(head * HEAD_DIM, (head + 1) * HEAD_DIM)
        top = jnp.full((1, ratio * rows), MASKED_SCORE, F32)
        for start in starts:
            scores = dot(kv_ref[start : start + CHUNK, span], queries, 1, 0)
            scores = scores + mask_bias(start, group_ref[0], key_ref, own_ref, rows, ratio)
            score_ref[start : start + CHUNK] = scores
            top = jnp.maximum(top, jnp.max(scores, axis=0, keepdims=True))
        total = jnp.zeros_like(top)
        mixed = jnp.zeros((HEAD_DIM, ratio * rows), F32)
        for start in starts:
            weights = jnp.exp(score_ref[start : start + CHUNK] - top)
            total = total + jnp.sum(weights, axis=0, keepdims=True)
            values = kv_ref[start : start + CHUNK, kv:][:, span]
            mixed = mixed + dot(values, weights.astype(BF), 0, 0)
        log_ref[head : head + 1] = top + jnp.log(total)
        mixed = (mixed / total).astype(BF)
        for i in range(ratio):
            at_head = (head * ratio + i) * HEAD_DIM
            out_ref[at_head : at_head + HEAD_DIM] = mixed[:, i * rows : (i + 1) * rows]


def attend_back_kernel(group_ref, q_ref, kv_ref, key_ref, own_ref, grad_ref, log_ref, cos_ref, sin_ref, gq_ref, gkv_ref, prob_ref, diff_ref):
    rows = q_ref.shape[1]
    length = kv_ref.shape[0]
    kv = kv_ref.shape[1] // 2
    ratio = q_ref.shape[0] // kv
    starts = range(0, length, CHUNK)
    cos, sin = cos_ref[...], sin_ref[...]
    grads_k, grads_v = [[], []], [[], []]
    for head in range(KV_HEADS):
        queries = heads_side_by_side(q_ref, head * ratio, ratio) * BF(HEAD_DIM**-0.5)
        grads = heads_side_by_side(grad_ref, head * ratio, ratio)
        span = slice(head * HEAD_DIM, (head + 1) * HEAD_DIM)
        log = log_ref[head : head + 1]
        inner = jnp.zeros((1, ratio * rows), F32)
        for start in starts:
            scores = dot(kv_ref[start : start + CHUNK, span], queries, 1, 0)
            scores = scores + mask_bias(start, group_ref[0], key_ref, own_ref, rows, ratio)
            probs = jnp.exp(scores - log)
            prob_ref[start : start + CHUNK] = probs
            diff = dot(kv_ref[start : start + CHUNK, kv:][:, span], grads, 1, 0)
            diff_ref[start : start + CHUNK] = diff
            inner = inner + jnp.sum(probs * diff, axis=0, keepdims=True)
        grad_q = jnp.zeros((HEAD_DIM, ratio * rows), F32)
        for start in starts:
            probs = prob_ref[start : start + CHUNK]
            grad_s = (probs * (diff_ref[start : start + CHUNK] - inner)).astype(BF)
            grads_k[head].append(dot(grad_s, queries, 1, 1))
            grads_v[head].append(dot(probs.astype(BF), grads, 1, 1))
            grad_q = grad_q + dot(kv_ref[start : start + CHUNK, span], grad_s, 0, 0)
        grad_q = grad_q * HEAD_DIM**-0.5
        blocks = []
        for i in range(ratio):
            blocks += turned_rows(grad_q[:, i * rows : (i + 1) * rows], cos, sin, True)
        lanes = ratio * HEAD_DIM
        gq_ref[:, head * lanes : (head + 1) * lanes] = jnp.concatenate(blocks).T.astype(BF)
    for i, start in enumerate(starts):
        parts = [grads_k[0][i], grads_k[1][i], grads_v[0][i], grads_v[1][i]]
        gkv_ref[start : start + CHUNK] = jnp.concatenate(parts, axis=1).astype(BF)


def tail_kernel(core_ref, arrived_ref, gq_ref, w_ref, x_ref, scale_ref, rows_ref, n_ref, mid_ref, cos_ref, sin_ref, in_ref, keep_ref, send_ref, g_ref, share_ref, line_ref, small_ref):
    rows, width = x_ref.shape
    lanes = w_ref.shape[1]
    kv = (lanes - width) // 2
    part = width // N
    total = arrived_ref[0].astype(F32)
    for j in range(1, N):
        total = total + arrived_ref[j].astype(F32)
    turned = total[:, :kv].T
    keys = []
    for h in range(KV_HEADS):
        block = turned[h * HEAD_DIM : (h + 1) * HEAD_DIM]
        keys += turned_rows(block, cos_ref[...], sin_ref[...], True)
    g_ref[:, :width] = gq_ref[...]
    g_ref[:, width : width + kv] = jnp.concatenate(keys).T.astype(BF)
    g_ref[:, width + kv :] = total[:, kv:].astype(BF)
    grads = g_ref[...]
    first = dot(grads, w_ref[...], 1, 1)
    scale = scale_ref[...]
    normalized = x_ref[...].astype(F32) * scale
    scaled = first * rows_ref[0:1, :width]
    mean = jnp.mean(scaled * normalized, axis=-1, keepdims=True)
    in_ref[...] = mid_ref[...] + scale * (scaled - normalized * mean)
    gain = jnp.sum(first * normalized, axis=0, keepdims=True)
    share_ref[...] = dot(n_ref[...], grads, 0, 0)
    bias = jnp.sum(grads.astype(F32), axis=0, keepdims=True)
    line_ref[0:1] = bias
    line_ref[1:2, :width] = gain
    small_ref[...] = jnp.zeros_like(small_ref)
    narrow = kv // N
    for j in range(N):
        at_lane = 0
        for row, start, count in (
            (0, part * j, part),
            (0, width + narrow * j, narrow),
            (0, width + kv + narrow * j, narrow),
            (1, part * j, part),
        ):
            piece = line_ref[row : row + 1, start : start + count]
            small_ref[j, 0:1, at_lane : at_lane + count] = piece
            at_lane += count

    def write(low, high):
        for j in range(N):
            low[j] = share_ref[part * j : part * j + HALF].astype(low.dtype)
            high[j, : part - HALF] = share_ref[part * j + HALF : part * (j + 1)].astype(high.dtype)
            high[j, part - HALF :] = small_ref[j].astype(high.dtype)

    @pl.when(core_ref[0] == 0)
    def _():
        write(keep_ref, send_ref)

    @pl.when(core_ref[0] != 0)
    def _():
        write(send_ref, keep_ref)


def pack_last(arrived_ref, down_ref, out_ref, columns_ref, sum_ref):
    width = out_ref.shape[2]
    lanes = sum_ref.shape[1] - width
    total = arrived_ref[0, :, : lanes + width].astype(F32)
    for j in range(1, N):
        total = total + arrived_ref[j, :, : lanes + width].astype(F32)
    sum_ref[...] = total.astype(BF)
    columns_ref[...] = arrived_ref[:, :48, lanes + width :]
    for p in range(6):
        out_ref[p, :48] = down_ref[48 * p : 48 * p + 48]
    out_ref[6, :32] = down_ref[288:320]
    out_ref[6, 32:48] = sum_ref[:16, lanes:]
    out_ref[7, :48] = sum_ref[16:HALF, lanes:]
    out_ref[:, 48:] = jnp.zeros((N, 16, width), BF)
    across = lanes // 128
    for i in range(4 * across):
        r, l = i // across, i % across
        tile = sum_ref[16 * r : 16 * r + 16, 128 * l : 128 * l + 128]
        out_ref[i // 5, 48:HALF, 128 * (i % 5) : 128 * (i % 5) + 128] = tile


def unpack_last(core_ref, own_ref, other_ref, down_ref, q_ref, k_ref, v_ref, out_ref, bq_ref, bk_ref, bv_ref, first_ref, second_ref):
    part, narrow = bq_ref.shape[1], bk_ref.shape[1]
    across = q_ref.shape[1] // 128 + 2

    def write(source, half):
        for p in range(6):
            start = 320 * half + 48 * p
            down_ref[start : start + 48] = source[p, :48].astype(F32)
        if half == 0:
            down_ref[288:320] = source[6, :32].astype(F32)
        first = HALF * half
        out_ref[first : first + 16] = source[6, 32:48].astype(F32)
        count = 48 - 16 * half
        out_ref[first + 16 : first + 16 + count] = source[7, :count].astype(F32)
        if half == 1:
            second_ref[...] = source[7, 32:48].astype(F32)[:1, :part]
        for i in range((4 - half) * across):
            r, l = i // across, i % across
            tile = source[i // 5, 48:HALF, 128 * (i % 5) : 128 * (i % 5) + 128].astype(F32)
            rows = slice(first + 16 * r, first + 16 * r + 16)
            if l < across - 2:
                q_ref[rows, 128 * l : 128 * l + 128] = tile
            elif l == across - 2:
                k_ref[rows] = tile
            else:
                v_ref[rows] = tile
        if half == 1:
            i = 3 * across
            line = [source[n // 5, 48:HALF, 128 * (n % 5) : 128 * (n % 5) + 128] for n in (i, i + 1)]
            line = jnp.concatenate(line, axis=1).astype(F32)[:1]
            bq_ref[...] = line[:, :part]
            bk_ref[...] = line[:, part : part + narrow]
            bv_ref[...] = line[:, part + narrow : part + 2 * narrow]
            first_ref[...] = line[:, part + 2 * narrow : 2 * part + 2 * narrow]

    @pl.when(core_ref[0] == 0)
    def _():
        write(own_ref, 0)
        write(other_ref, 1)

    @pl.when(core_ref[0] != 0)
    def _():
        write(other_ref, 0)
        write(own_ref, 1)


def halves_of(ref, half):
    block = ref[:, half * HALF : (half + 1) * HALF]
    return block.reshape(-1, ref.shape[2])


def feed_forward(half, x_ref, cot_ref, gu_ref, dn_ref, second_ref, down_ref, hidden_ref, grad_ref):
    step = 4
    for at_block in range(0, N, step):
        x = x_ref[at_block : at_block + step].reshape(step * HALF, -1)
        cot = cot_ref[at_block : at_block + step, half * HALF : (half + 1) * HALF]
        cot = cot.reshape(step * HALF, -1)
        gate = dot(x, gu_ref[:, :PAD], 1, 0)
        up = dot(x, gu_ref[:, PAD:], 1, 0)
        back = dot(cot, dn_ref[...], 1, 1)
        sigmoid = jax.nn.sigmoid(gate)
        silu = gate * sigmoid
        hidden = (silu * up).astype(BF)
        grad_gate = (back * up * sigmoid * (1.0 + gate * (1.0 - sigmoid))).astype(BF)
        grad_up = (back * silu).astype(BF)
        span = slice(at_block * HALF, (at_block + step) * HALF)
        hidden_ref[span] = hidden
        grad_ref[span, :PAD] = grad_gate
        grad_ref[span, PAD:] = grad_up
        second = dot(grad_gate, gu_ref[:, :PAD], 1, 1) + dot(grad_up, gu_ref[:, PAD:], 1, 1)
        second_ref[at_block : at_block + step] = second.astype(BF).reshape(step, HALF, -1)
        down = dot(hidden, dn_ref[...], 1, 0)
        down_ref[at_block : at_block + step] = down.astype(BF).reshape(step, HALF, -1)


def unit_weight_grads(core_ref, xa_ref, xb_ref, ga_ref, gb_ref, keep_ref, send_ref):
    xa, xb = xa_ref[...].reshape(N * HALF, -1), xb_ref[...].reshape(N * HALF, -1)
    for side, target in ((core_ref[0], keep_ref), (1 - core_ref[0], send_ref)):
        span = pl.ds(pl.multiple_of(side * PAD, 128), PAD)
        grad = dot(xa, ga_ref[:, span], 0, 0) + dot(xb, gb_ref[:, span], 0, 0)
        target[...] = grad.astype(target.dtype)


def down_weight_grads(core_ref, ha_ref, hb_ref, cot_ref, keep_ref, send_ref, grad_ref):
    grad_ref[...] = dot(ha_ref[...], halves_of(cot_ref, 0), 0, 0) + dot(
        hb_ref[...], halves_of(cot_ref, 1), 0, 0
    )
    count = PAD // 2
    for side, target in ((core_ref[0], keep_ref), (1 - core_ref[0], send_ref)):
        span = pl.ds(pl.multiple_of(side * count, 64), count)
        target[...] = grad_ref[span].astype(target.dtype)


def shape(dtype, *dims):
    return jax.ShapeDtypeStruct(dims, dtype)


def local(
    hidden_in,
    segment_ids,
    attn_gain,
    w_query,
    b_query,
    w_key,
    b_key,
    w_value,
    b_value,
    w_out,
    ffn_gain,
    w_gate,
    w_up,
    w_down,
    cotangent,
):
    g = lax.axis_index(GROUP)
    c = lax.axis_index("c")
    rows, width = hidden_in.shape[1:]
    part = w_query.shape[1]
    units = w_down.shape[1]
    kv = w_key.shape[2]
    heads = width // HEAD_DIM

    lanes = width + 2 * kv
    k16 = kv // N
    core, group = c.reshape(1), g.reshape(1)

    def spread_out(vector):
        place = jnp.arange(N * vector.shape[0]) // vector.shape[0] == g
        return jnp.where(place, jnp.tile(vector, N), BF(0))

    bias = [spread_out(b[0]) for b in (b_query, b_key, b_value)]
    blank = jnp.zeros((2 * kv,), BF)
    small = jnp.stack(
        [
            jnp.concatenate([spread_out(attn_gain[0]), blank]),
            jnp.concatenate(bias),
            jnp.concatenate([spread_out(ffn_gain[0]), blank]),
        ]
    )
    small = jnp.pad(small, ((0, 13), (0, 0)))
    z, xh = lax.axis_index("z"), lax.axis_index("xh")
    place = jnp.stack([c, z, xh]).astype(jnp.int32)
    halves = call(
        pack_weights,
        shape(BF, N, HALF, lanes + SIDE),
        place,
        w_query[0],
        w_key[0],
        w_value[0],
        small,
        w_gate[0],
        w_up[0],
        scalars=1,
    )
    own_half = exchange(halves, GROUP)
    own_half, w_out, cotangent = lax.optimization_barrier((own_half, w_out, cotangent))
    other_half = shift(own_half, "c", 1, 2)
    group_down = lax.all_gather(cotangent[0], GROUP, axis=0, tiled=True).reshape(N, rows, width)
    out_half = to_all(at(w_out[0].reshape(2, part // 2, width), c), GROUP)
    other_half = shift(own_half, "c", 1, 2)

    segments = segment_ids[0]
    length = segments.shape[0]
    own_segments = lax.dynamic_slice_in_dim(segments, g * rows, rows, 0)
    query_index = g * rows + jnp.arange(rows, dtype=jnp.int32)
    earlier = jnp.sum((segments[None, :] < own_segments[:, None]).astype(jnp.int32), axis=-1)
    positions = query_index - earlier
    half = HEAD_DIM // 2
    frequency = THETA ** (-(2.0 * jnp.arange(half, dtype=F32)) / HEAD_DIM)
    angles = positions.astype(F32)[None, :] * frequency[:, None]
    cosine, sine = jnp.cos(angles), jnp.sin(angles)
    key_segments, own_segments = segments[:, None], own_segments[None]

    w_qkv, gains, queries, own_kv, normed, first_scale = call(
        project_tokens,
        (
            shape(BF, width, lanes),
            shape(F32, 16, lanes),
            shape(BF, width, rows),
            shape(BF, rows, 2 * kv),
            shape(BF, rows, width),
            shape(F32, rows, 1),
        ),
        core,
        hidden_in[0],
        own_half,
        other_half,
        cosine,
        sine,
        scalars=1,
    )
    second_gain = gains[2, :width]
    out_half, own_kv = lax.optimization_barrier((out_half, own_kv))
    all_kv = to_all(own_kv, GROUP).reshape(length, 2 * kv)

    out_weight = jnp.stack(core_pair(out_half, c), axis=1).reshape(width, width)
    piece = own_half[:, :, lanes:]
    pieces = jnp.stack([shift(piece, "z", -k, 4) for k in (1, 2, 3)])
    w_gu = call(
        join_units,
        shape(BF, width, 2 * PAD),
        place,
        own_half,
        other_half,
        pieces,
        shift(pieces, "c", 1, 2),
        scalars=1,
    )
    w_dn = jnp.pad(w_down[0], ((0, PAD - units), (0, 0)))

    wide = heads // KV_HEADS * rows
    attended, logsum = call(
        attend_kernel,
        (shape(BF, width, rows), shape(F32, KV_HEADS, wide)),
        group,
        queries,
        all_kv,
        key_segments,
        own_segments,
        scalars=1,
        scratch=[((length, wide), F32)],
    )
    stream = hidden_in[0].astype(F32)
    middle = stream + outer(attended, out_weight)

    second_normed, second_scale = norm_forward(middle, second_gain)
    second_normed = second_normed.astype(BF)
    inputs, hiddens, grads, seconds, downs = [], [], [], [], []
    for half in range(2):
        gathered = to_all(second_normed[half * HALF : (half + 1) * HALF], GROUP)
        second, down, hidden, grad = call(
            functools.partial(feed_forward, half),
            (
                shape(BF, N, HALF, width),
                shape(BF, N, HALF, width),
                shape(BF, N * HALF, PAD),
                shape(BF, N * HALF, 2 * PAD),
            ),
            gathered,
            group_down,
            w_gu,
            w_dn,
            flops=12 * N * HALF * width * PAD,
        )
        inputs.append(gathered)
        hiddens.append(hidden)
        grads.append(grad)
        seconds.append(second)
        downs.append(down)
    first_return = exchange(seconds[0], GROUP)
    second_return = exchange(seconds[1], GROUP)
    first_return, grads, hiddens = lax.optimization_barrier((first_return, grads, hiddens))

    cost = 4 * length * width * PAD
    unit_keep, unit_send = call(
        unit_weight_grads,
        (shape(F32, width, PAD), shape(BF, width, PAD)),
        core,
        *inputs,
        *grads,
        scalars=1,
        flops=cost,
    )
    down_keep, down_send = call(
        down_weight_grads,
        (shape(F32, PAD // 2, width), shape(BF, PAD // 2, width)),
        core,
        *hiddens,
        group_down,
        scalars=1,
        scratch=[((PAD, width), F32)],
        flops=cost // 2,
    )
    second_return, unit_send, down_send = lax.optimization_barrier(
        (second_return, unit_send, down_send)
    )
    grad_second = jnp.concatenate(
        [jnp.sum(part_sum.astype(F32), axis=0) for part_sum in (first_return, second_return)]
    )
    unit_share = (unit_keep + shift(unit_send, "c", 1, 2).astype(F32)).astype(BF)
    down_share = (down_keep + shift(down_send, "c", 1, 2).astype(F32)).astype(BF)
    blocks = unit_share.reshape(N, part // 16, 16, PAD)
    blocks = jnp.pad(blocks, ((0, 0), (0, N - part // 16), (0, 0), (0, 0)))
    blocks = jnp.moveaxis(blocks, 1, 0).reshape(2, 4, N, 16, PAD)

    def along_z(k):
        return lax.dynamic_index_in_dim(blocks, (z + k) % 4, 1, keepdims=False)

    unit_share = along_z(0).astype(F32)
    for k in (1, 3, 2):
        unit_share = unit_share + shift(along_z(k), "z", k, 4).astype(F32)

    grad_second, downs = lax.optimization_barrier((grad_second, downs))
    down_arrived = exchange(jnp.concatenate(downs, axis=1), GROUP)

    stream_grad = cotangent[0].astype(F32)
    term, gain_second = norm_backward(middle, second_scale, second_gain, grad_second)
    grad_middle = stream_grad + term
    attn_grad = grad_middle.astype(BF)
    grad_attended = mm_t(out_weight, attn_grad).astype(BF)
    small = jnp.pad(gain_second.reshape(N, 1, part), ((0, 0), (0, 15), (0, width - part)))
    grad_out = mm(attended, attn_grad).reshape(N, part, width)
    grad_out = jnp.concatenate([grad_out, small], axis=1)
    out_share = core_sum(grad_out[:, :HALF], grad_out[:, HALF:], c)
    grad_q, grad_kv = call(
        attend_back_kernel,
        (shape(BF, rows, width), shape(BF, length, 2 * kv)),
        group,
        queries,
        all_kv,
        key_segments,
        own_segments,
        grad_attended,
        logsum,
        cosine,
        sine,
        scalars=1,
        scratch=[((length, wide), F32)] * 2,
    )
    grad_kv, unit_share, down_arrived = lax.optimization_barrier((grad_kv, unit_share, down_arrived))
    arrived = exchange(grad_kv.reshape(N, rows, 2 * kv), GROUP)

    sent = shift(at(unit_share, 1 - xh).astype(BF), "xh", 1, 2)
    unit_share = (at(unit_share, xh) + sent.astype(F32)).astype(BF)
    tiles = [unit_share[:, :, 128 * t : 128 * (t + 1)] for t in range(5)]
    tiles += [jnp.zeros_like(tiles[0])] * 3
    tiles = [jnp.concatenate(tiles[2 * i : 2 * i + 2], axis=2) for i in range(4)]
    unit_share = jnp.concatenate(tiles, axis=1)
    arrived, out_share = lax.optimization_barrier((arrived, out_share))

    grad_in, keep, send = call(
        tail_kernel,
        (shape(F32, rows, width), shape(F32, N, HALF, lanes), shape(BF, N, HALF, lanes)),
        core,
        arrived,
        grad_q,
        w_qkv,
        hidden_in[0],
        first_scale,
        gains,
        normed,
        grad_middle,
        cosine,
        sine,
        scalars=1,
        scratch=[((rows, lanes), BF), ((width, lanes), F32), ((8, lanes), F32), ((N, 16, lanes), F32)],
    )
    grad_in = grad_in[None]
    share = (keep + shift(send, "c", 1, 2).astype(F32)).astype(BF)
    share, unit_share, down_arrived = lax.optimization_barrier((share, unit_share, down_arrived))
    arrived = exchange(jnp.concatenate([share, out_share, unit_share], axis=2), GROUP)
    layer_out = middle + jnp.sum(down_arrived.astype(F32), axis=0)
    hidden_out = layer_out.astype(BF)[None]
    share, columns = call(
        pack_last,
        (shape(BF, N, HALF, width), shape(BF, N, 48, 256)),
        arrived,
        down_share,
        scratch=[((HALF, lanes + width), BF)],
    )
    columns = jnp.stack([columns, shift(columns, "xh", 1, 2)])
    columns = jnp.stack([columns] + [shift(columns, "z", -k, 4) for k in (1, 2, 3)])

    share = to_all(sum_at(share, SPREAD).astype(BF), SPREAD)
    other_columns = shift(columns, "c", 1, 2)
    share, other_columns = lax.optimization_barrier((share, other_columns))
    other_share = shift(share, "c", 1, 2)
    units_out = (shape(F32, part, N * units),) * 2
    units_out = call(
        unpack_units, units_out, place, columns, other_columns, scalars=1
    )
    grad_w_gate, grad_w_up = [grad[None] for grad in units_out]
    narrow = [shape(F32, 1, count) for count in (part, k16, k16, part, part)]
    down, w_q, w_k, w_v, w_o, b_q, b_k, b_v, first, second = call(
        unpack_last,
        (
            shape(F32, units, width),
            shape(F32, part, width),
            shape(F32, part, kv),
            shape(F32, part, kv),
            shape(F32, part, width),
            *narrow,
        ),
        core,
        share,
        other_share,
        scalars=1,
    )
    weights = (first, w_q[None], b_q, w_k[None], b_k, w_v[None], b_v, w_o[None], second)
    return (hidden_out, grad_in) + weights + (grad_w_gate, grad_w_up, down[None])


def solution(mesh):
    split = Mesh(mesh.devices.reshape(SIZES), AXES)
    tokens = P(REPLICA, GROUP, None)
    vector = P(None, GROUP)
    matrix = P(None, GROUP, None)
    weights = (vector, matrix, vector, matrix, vector, matrix, vector, matrix, vector)
    return jax.shard_map(
        local,
        mesh=split,
        in_specs=(tokens, P(REPLICA, None)) + weights + (matrix,) * 3 + (tokens,),
        out_specs=(tokens, tokens) + weights + (matrix,) * 3,
        check_vma=False,
    )
```

```python
import functools

import jax
import jax.numpy as jnp
from jax import lax
from jax.experimental import pallas as pl
from jax.experimental.pallas import tpu as pltpu
from jax.sharding import Mesh
from jax.sharding import PartitionSpec as P

KV_HEADS = 2
HEAD_DIM = 64
EPS = 1e-06
THETA = 1000000.0
MASKED_SCORE = -1e30
GROUP = ("y", "xl")
SPREAD = ("xh", "z")
REPLICA = ("xh", "z", "c")
SIZES = (4, 2, 2, 4, 2)
AXES = ("y", "xl", "xh", "z", "c")
N = 8
PAD = 640
HALF = 64
BF = jnp.bfloat16
F32 = jnp.float32


def shift(array, axis, by, size):
    return lax.ppermute(array, axis, [(i, (i + by) % size) for i in range(size)])


def exchange(blocks, axis):
    return lax.all_to_all(blocks, axis, 0, 0, tiled=True)


def to_all(array, axis):
    return exchange(jnp.broadcast_to(array, (N, *array.shape)), axis)


def sum_at(blocks, axis):
    return jnp.sum(exchange(blocks, axis).astype(F32), axis=0)


def at(blocks, index):
    return lax.dynamic_index_in_dim(blocks, index, 0, keepdims=False)


def norm_forward(stream, gain):
    scale = lax.rsqrt(jnp.mean(stream * stream, axis=-1, keepdims=True) + EPS)
    return stream * scale * gain, scale


def norm_backward(stream, scale, gain, gradient):
    normalized = stream * scale
    scaled = gradient * gain
    gain_grad = jnp.sum(gradient * normalized, axis=0)
    grad = scale * (scaled - normalized * jnp.mean(scaled * normalized, axis=-1, keepdims=True))
    return grad, gain_grad


def mm(a, b):
    return jnp.dot(a, b, preferred_element_type=F32)


def mm_t(a, b):
    return lax.dot_general(a, b, (((1,), (1,)), ((), ())), preferred_element_type=F32)


def outer(a, b):
    return lax.dot_general(a, b, (((0,), (0,)), ((), ())), preferred_element_type=F32)


def core_sum(first, second, c):
    low = c == 0
    keep = jnp.where(low, first, second)
    send = jnp.where(low, second, first).astype(BF)
    return (keep + shift(send, "c", 1, 2).astype(F32)).astype(BF)


def core_pair(own, c):
    other = shift(own, "c", 1, 2)
    low = c == 0
    return jnp.where(low, own, other), jnp.where(low, other, own)


def unpack_units(place_ref, own_ref, other_ref, gate_ref, up_ref):
    units = gate_ref.shape[1] // N
    c, z, xh = place_ref[0], place_ref[1], place_ref[2]

    def write(source, target):
        for piece in range(target.shape[0] // 16):
            slot = lax.rem(piece % 4 + 4 - z, 4)
            second = lax.rem(xh + piece // 4, 2)
            for j in range(N):
                for t in range(5):
                    count = min(128, units - 128 * t)
                    row, lane = 16 * (t // 2), 128 * (t % 2)
                    tile = source[slot, second, j, row : row + 16, lane : lane + count]
                    start = units * j + 128 * t
                    target[16 * piece : 16 * piece + 16, start : start + count] = tile.astype(F32)

    @pl.when(c == 0)
    def _():
        write(own_ref, gate_ref)
        write(other_ref, up_ref)

    @pl.when(c != 0)
    def _():
        write(other_ref, gate_ref)
        write(own_ref, up_ref)


VMEM = pl.BlockSpec(memory_space=pltpu.VMEM)
SMEM = pl.BlockSpec(memory_space=pltpu.SMEM)


def call(kernel, outs, *args, scalars=0, scratch=(), flops=0, mib=48):
    cost = pl.CostEstimate(flops=flops, bytes_accessed=2**20, transcendentals=0)
    return pl.pallas_call(
        kernel,
        out_shape=outs,
        in_specs=[SMEM] * scalars + [VMEM] * (len(args) - scalars),
        out_specs=jax.tree.map(lambda _: VMEM, outs),
        scratch_shapes=[pltpu.VMEM(shape, dtype) for shape, dtype in scratch],
        compiler_params=pltpu.CompilerParams(vmem_limit_bytes=mib * 2**20),
        cost_estimate=cost,
    )(*args)


SIDE = 384


def pack_weights(place_ref, q_ref, k_ref, v_ref, row_ref, gate_ref, up_ref, out_ref):
    part = q_ref.shape[0]
    width, kv = q_ref.shape[1], k_ref.shape[1]
    lanes = width + 2 * kv
    units = gate_ref.shape[1] // N
    spans = ((0, q_ref), (width, k_ref), (width + kv, v_ref))
    out_ref[:, :, lanes:] = jnp.zeros((N, HALF, SIDE), BF)
    first = pl.multiple_of(piece_start(place_ref[1], part), 16)

    def beside(ref):
        for j in range(N):
            for t in range(5):
                count = min(128, units - 128 * t)
                start = units * j + 128 * t
                row, lane = 32 * (t // 3), lanes + 128 * (t % 3)
                tile = ref[pl.ds(first, 32), start : start + count]
                out_ref[j, row : row + 32, lane : lane + count] = tile

    @pl.when(place_ref[0] == 0)
    def _():
        beside(gate_ref)
        for j in range(N):
            for start, ref in spans:
                out_ref[j, :, start : start + ref.shape[1]] = ref[:HALF]

    @pl.when(place_ref[0] != 0)
    def _():
        beside(up_ref)
        for j in range(N):
            for start, ref in spans:
                out_ref[j, : part - HALF, start : start + ref.shape[1]] = ref[HALF:]
            out_ref[j, part - HALF :, :lanes] = row_ref[...]


def piece_start(z, part):
    return jnp.minimum(32 * z, part - 32)


def join_units(place_ref, own_ref, other_ref, own_z_ref, other_z_ref, w_ref):
    part = w_ref.shape[0] // N
    lanes = own_ref.shape[2] - SIDE
    z = place_ref[1]

    def write(sources, side):
        near, far = sources

        @pl.loop(0, N)
        def _(j):
            for k in range(4):
                start = part * j + piece_start(lax.rem(z + k, 4), part)
                rows = pl.ds(pl.multiple_of(start, 16), 32)
                for t in range(5):
                    row, lane = 32 * (t // 3), 128 * (t % 3)
                    if k == 0:
                        tile = near[j, row : row + 32, lanes + lane : lanes + lane + 128]
                    else:
                        tile = far[k - 1, j, row : row + 32, lane : lane + 128]
                    column = side * PAD + 128 * t
                    w_ref[rows, column : column + 128] = tile

    @pl.when(place_ref[0] == 0)
    def _():
        write((own_ref, own_z_ref), 0)
        write((other_ref, other_z_ref), 1)

    @pl.when(place_ref[0] != 0)
    def _():
        write((own_ref, own_z_ref), 1)
        write((other_ref, other_z_ref), 0)


def dot(a, b, da, db):
    return lax.dot_general(a, b, (((da,), (db,)), ((), ())), preferred_element_type=F32)


def turned_rows(block, cos, sin, back):
    half = HEAD_DIM // 2
    top, low = block[:half], block[half:]
    if back:
        return [top * cos + low * sin, low * cos - top * sin]
    return [top * cos - low * sin, low * cos + top * sin]


def project_tokens(core_ref, x_ref, own_ref, other_ref, cos_ref, sin_ref, w_ref, rows_ref, q_ref, kv_ref, n_ref, scale_ref):
    part = w_ref.shape[0] // N
    width = x_ref.shape[1]
    lanes = w_ref.shape[1]
    kv = (lanes - width) // 2

    def assemble(low, high):
        small = jnp.zeros((16, lanes), F32)
        for j in range(N):
            w_ref[part * j : part * j + HALF] = low[j, :, :lanes]
            w_ref[part * j + HALF : part * (j + 1)] = high[j, : part - HALF, :lanes]
            small = small + high[j, part - HALF :, :lanes].astype(F32)
        rows_ref[...] = small

    @pl.when(core_ref[0] == 0)
    def _():
        assemble(own_ref, other_ref)

    @pl.when(core_ref[0] != 0)
    def _():
        assemble(other_ref, own_ref)

    x = x_ref[...].astype(F32)
    scale = lax.rsqrt(jnp.mean(x * x, axis=-1, keepdims=True) + EPS)
    scale_ref[...] = scale
    normed = (x * scale * rows_ref[0:1, :width]).astype(BF)
    n_ref[...] = normed
    raw = dot(normed, w_ref[...], 1, 0) + rows_ref[1:2, :]
    kv_ref[:, kv:] = raw[:, width + kv :].astype(BF)
    turned = raw[:, : width + kv].T
    cos, sin = cos_ref[...], sin_ref[...]
    for h in range(width // HEAD_DIM):
        block = turned[h * HEAD_DIM : (h + 1) * HEAD_DIM]
        q_ref[h * HEAD_DIM : (h + 1) * HEAD_DIM] = jnp.concatenate(
            turned_rows(block, cos, sin, False)
        ).astype(BF)
    keys = []
    for h in range(width // HEAD_DIM, (width + kv) // HEAD_DIM):
        keys += turned_rows(turned[h * HEAD_DIM : (h + 1) * HEAD_DIM], cos, sin, False)
    kv_ref[:, :kv] = jnp.concatenate(keys).T.astype(BF)


CHUNK = 256


def heads_side_by_side(ref, first, ratio):
    return jnp.concatenate(
        [ref[(first + i) * HEAD_DIM : (first + i + 1) * HEAD_DIM] for i in range(ratio)], axis=1
    )


def mask_bias(start, group, key_ref, own_ref, rows, ratio):
    key = start + lax.broadcasted_iota(jnp.int32, (CHUNK, rows), 0)
    query = group * rows + lax.broadcasted_iota(jnp.int32, (CHUNK, rows), 1)
    allowed = (key <= query) & (key_ref[start : start + CHUNK] == own_ref[...])
    bias = jnp.where(allowed, 0.0, MASKED_SCORE)
    return jnp.concatenate([bias] * ratio, axis=1)


def attend_kernel(group_ref, q_ref, kv_ref, key_ref, own_ref, out_ref, log_ref, score_ref):
    rows = q_ref.shape[1]
    length = kv_ref.shape[0]
    kv = kv_ref.shape[1] // 2
    ratio = q_ref.shape[0] // kv
    starts = range(0, length, CHUNK)
    for head in range(KV_HEADS):
        queries = heads_side_by_side(q_ref, head * ratio, ratio) * BF(HEAD_DIM**-0.5)
        span = slice(head * HEAD_DIM, (head + 1) * HEAD_DIM)
        top = jnp.full((1, ratio * rows), MASKED_SCORE, F32)
        for start in starts:
            scores = dot(kv_ref[start : start + CHUNK, span], queries, 1, 0)
            scores = scores + mask_bias(start, group_ref[0], key_ref, own_ref, rows, ratio)
            score_ref[start : start + CHUNK] = scores
            top = jnp.maximum(top, jnp.max(scores, axis=0, keepdims=True))
        total = jnp.zeros_like(top)
        mixed = jnp.zeros((HEAD_DIM, ratio * rows), F32)
        for start in starts:
            weights = jnp.exp(score_ref[start : start + CHUNK] - top)
            total = total + jnp.sum(weights, axis=0, keepdims=True)
            values = kv_ref[start : start + CHUNK, kv:][:, span]
            mixed = mixed + dot(values, weights.astype(BF), 0, 0)
        log_ref[head : head + 1] = top + jnp.log(total)
        mixed = (mixed / total).astype(BF)
        for i in range(ratio):
            at_head = (head * ratio + i) * HEAD_DIM
            out_ref[at_head : at_head + HEAD_DIM] = mixed[:, i * rows : (i + 1) * rows]


def attend_back_kernel(group_ref, q_ref, kv_ref, key_ref, own_ref, grad_ref, log_ref, cos_ref, sin_ref, gq_ref, gkv_ref, prob_ref, diff_ref):
    rows = q_ref.shape[1]
    length = kv_ref.shape[0]
    kv = kv_ref.shape[1] // 2
    ratio = q_ref.shape[0] // kv
    starts = range(0, length, CHUNK)
    cos, sin = cos_ref[...], sin_ref[...]
    grads_k, grads_v = [[], []], [[], []]
    for head in range(KV_HEADS):
        queries = heads_side_by_side(q_ref, head * ratio, ratio) * BF(HEAD_DIM**-0.5)
        grads = heads_side_by_side(grad_ref, head * ratio, ratio)
        span = slice(head * HEAD_DIM, (head + 1) * HEAD_DIM)
        log = log_ref[head : head + 1]
        inner = jnp.zeros((1, ratio * rows), F32)
        for start in starts:
            scores = dot(kv_ref[start : start + CHUNK, span], queries, 1, 0)
            scores = scores + mask_bias(start, group_ref[0], key_ref, own_ref, rows, ratio)
            probs = jnp.exp(scores - log)
            prob_ref[start : start + CHUNK] = probs
            diff = dot(kv_ref[start : start + CHUNK, kv:][:, span], grads, 1, 0)
            diff_ref[start : start + CHUNK] = diff
            inner = inner + jnp.sum(probs * diff, axis=0, keepdims=True)
        grad_q = jnp.zeros((HEAD_DIM, ratio * rows), F32)
        for start in starts:
            probs = prob_ref[start : start + CHUNK]
            grad_s = (probs * (diff_ref[start : start + CHUNK] - inner)).astype(BF)
            grads_k[head].append(dot(grad_s, queries, 1, 1))
            grads_v[head].append(dot(probs.astype(BF), grads, 1, 1))
            grad_q = grad_q + dot(kv_ref[start : start + CHUNK, span], grad_s, 0, 0)
        grad_q = grad_q * HEAD_DIM**-0.5
        blocks = []
        for i in range(ratio):
            blocks += turned_rows(grad_q[:, i * rows : (i + 1) * rows], cos, sin, True)
        lanes = ratio * HEAD_DIM
        gq_ref[:, head * lanes : (head + 1) * lanes] = jnp.concatenate(blocks).T.astype(BF)
    for i, start in enumerate(starts):
        parts = [grads_k[0][i], grads_k[1][i], grads_v[0][i], grads_v[1][i]]
        gkv_ref[start : start + CHUNK] = jnp.concatenate(parts, axis=1).astype(BF)


def tail_kernel(core_ref, arrived_ref, gq_ref, w_ref, x_ref, scale_ref, rows_ref, n_ref, mid_ref, cos_ref, sin_ref, in_ref, keep_ref, send_ref, g_ref, share_ref, line_ref, small_ref):
    rows, width = x_ref.shape
    lanes = w_ref.shape[1]
    kv = (lanes - width) // 2
    part = width // N
    total = arrived_ref[0].astype(F32)
    for j in range(1, N):
        total = total + arrived_ref[j].astype(F32)
    turned = total[:, :kv].T
    keys = []
    for h in range(KV_HEADS):
        block = turned[h * HEAD_DIM : (h + 1) * HEAD_DIM]
        keys += turned_rows(block, cos_ref[...], sin_ref[...], True)
    g_ref[:, :width] = gq_ref[...]
    g_ref[:, width : width + kv] = jnp.concatenate(keys).T.astype(BF)
    g_ref[:, width + kv :] = total[:, kv:].astype(BF)
    grads = g_ref[...]
    first = dot(grads, w_ref[...], 1, 1)
    scale = scale_ref[...]
    normalized = x_ref[...].astype(F32) * scale
    scaled = first * rows_ref[0:1, :width]
    mean = jnp.mean(scaled * normalized, axis=-1, keepdims=True)
    in_ref[...] = mid_ref[...] + scale * (scaled - normalized * mean)
    gain = jnp.sum(first * normalized, axis=0, keepdims=True)
    share_ref[...] = dot(n_ref[...], grads, 0, 0)
    bias = jnp.sum(grads.astype(F32), axis=0, keepdims=True)
    line_ref[0:1] = bias
    line_ref[1:2, :width] = gain
    small_ref[...] = jnp.zeros_like(small_ref)
    narrow = kv // N
    for j in range(N):
        at_lane = 0
        for row, start, count in (
            (0, part * j, part),
            (0, width + narrow * j, narrow),
            (0, width + kv + narrow * j, narrow),
            (1, part * j, part),
        ):
            piece = line_ref[row : row + 1, start : start + count]
            small_ref[j, 0:1, at_lane : at_lane + count] = piece
            at_lane += count

    def write(low, high):
        for j in range(N):
            low[j] = share_ref[part * j : part * j + HALF].astype(low.dtype)
            high[j, : part - HALF] = share_ref[part * j + HALF : part * (j + 1)].astype(high.dtype)
            high[j, part - HALF :] = small_ref[j].astype(high.dtype)

    @pl.when(core_ref[0] == 0)
    def _():
        write(keep_ref, send_ref)

    @pl.when(core_ref[0] != 0)
    def _():
        write(send_ref, keep_ref)


def pack_last(arrived_ref, down_ref, out_ref, columns_ref, sum_ref):
    width = out_ref.shape[2]
    lanes = sum_ref.shape[1] - width
    total = arrived_ref[0, :, : lanes + width].astype(F32)
    for j in range(1, N):
        total = total + arrived_ref[j, :, : lanes + width].astype(F32)
    sum_ref[...] = total.astype(BF)
    columns_ref[...] = arrived_ref[:, :48, lanes + width :]
    for p in range(6):
        out_ref[p, :48] = down_ref[48 * p : 48 * p + 48]
    out_ref[6, :32] = down_ref[288:320]
    out_ref[6, 32:48] = sum_ref[:16, lanes:]
    out_ref[7, :48] = sum_ref[16:HALF, lanes:]
    out_ref[:, 48:] = jnp.zeros((N, 16, width), BF)
    across = lanes // 128
    for i in range(4 * across):
        r, l = i // across, i % across
        tile = sum_ref[16 * r : 16 * r + 16, 128 * l : 128 * l + 128]
        out_ref[i // 5, 48:HALF, 128 * (i % 5) : 128 * (i % 5) + 128] = tile


def unpack_last(core_ref, own_ref, other_ref, down_ref, q_ref, k_ref, v_ref, out_ref, bq_ref, bk_ref, bv_ref, first_ref, second_ref):
    part, narrow = bq_ref.shape[1], bk_ref.shape[1]
    across = q_ref.shape[1] // 128 + 2

    def write(source, half):
        for p in range(6):
            start = 320 * half + 48 * p
            down_ref[start : start + 48] = source[p, :48].astype(F32)
        if half == 0:
            down_ref[288:320] = source[6, :32].astype(F32)
        first = HALF * half
        out_ref[first : first + 16] = source[6, 32:48].astype(F32)
        count = 48 - 16 * half
        out_ref[first + 16 : first + 16 + count] = source[7, :count].astype(F32)
        if half == 1:
            second_ref[...] = source[7, 32:48].astype(F32)[:1, :part]
        for i in range((4 - half) * across):
            r, l = i // across, i % across
            tile = source[i // 5, 48:HALF, 128 * (i % 5) : 128 * (i % 5) + 128].astype(F32)
            rows = slice(first + 16 * r, first + 16 * r + 16)
            if l < across - 2:
                q_ref[rows, 128 * l : 128 * l + 128] = tile
            elif l == across - 2:
                k_ref[rows] = tile
            else:
                v_ref[rows] = tile
        if half == 1:
            i = 3 * across
            line = [source[n // 5, 48:HALF, 128 * (n % 5) : 128 * (n % 5) + 128] for n in (i, i + 1)]
            line = jnp.concatenate(line, axis=1).astype(F32)[:1]
            bq_ref[...] = line[:, :part]
            bk_ref[...] = line[:, part : part + narrow]
            bv_ref[...] = line[:, part + narrow : part + 2 * narrow]
            first_ref[...] = line[:, part + 2 * narrow : 2 * part + 2 * narrow]

    @pl.when(core_ref[0] == 0)
    def _():
        write(own_ref, 0)
        write(other_ref, 1)

    @pl.when(core_ref[0] != 0)
    def _():
        write(other_ref, 0)
        write(own_ref, 1)


def halves_of(ref, half):
    block = ref[:, half * HALF : (half + 1) * HALF]
    return block.reshape(-1, ref.shape[2])


def feed_forward(half, x_ref, cot_ref, gu_ref, dn_ref, second_ref, down_ref, hidden_ref, grad_ref):
    step = 4
    for at_block in range(0, N, step):
        x = x_ref[at_block : at_block + step].reshape(step * HALF, -1)
        cot = cot_ref[at_block : at_block + step, half * HALF : (half + 1) * HALF]
        cot = cot.reshape(step * HALF, -1)
        gate = dot(x, gu_ref[:, :PAD], 1, 0)
        up = dot(x, gu_ref[:, PAD:], 1, 0)
        back = dot(cot, dn_ref[...], 1, 1)
        sigmoid = jax.nn.sigmoid(gate)
        silu = gate * sigmoid
        hidden = (silu * up).astype(BF)
        grad_gate = (back * up * sigmoid * (1.0 + gate * (1.0 - sigmoid))).astype(BF)
        grad_up = (back * silu).astype(BF)
        span = slice(at_block * HALF, (at_block + step) * HALF)
        hidden_ref[span] = hidden
        grad_ref[span, :PAD] = grad_gate
        grad_ref[span, PAD:] = grad_up
        second = dot(grad_gate, gu_ref[:, :PAD], 1, 1) + dot(grad_up, gu_ref[:, PAD:], 1, 1)
        second_ref[at_block : at_block + step] = second.astype(BF).reshape(step, HALF, -1)
        down = dot(hidden, dn_ref[...], 1, 0)
        down_ref[at_block : at_block + step] = down.astype(BF).reshape(step, HALF, -1)


def unit_weight_grads(core_ref, xa_ref, xb_ref, ga_ref, gb_ref, keep_ref, send_ref):
    xa, xb = xa_ref[...].reshape(N * HALF, -1), xb_ref[...].reshape(N * HALF, -1)
    for side, target in ((core_ref[0], keep_ref), (1 - core_ref[0], send_ref)):
        span = pl.ds(pl.multiple_of(side * PAD, 128), PAD)
        grad = dot(xa, ga_ref[:, span], 0, 0) + dot(xb, gb_ref[:, span], 0, 0)
        target[...] = grad.astype(target.dtype)


def down_weight_grads(core_ref, ha_ref, hb_ref, cot_ref, keep_ref, send_ref, grad_ref):
    grad_ref[...] = dot(ha_ref[...], halves_of(cot_ref, 0), 0, 0) + dot(
        hb_ref[...], halves_of(cot_ref, 1), 0, 0
    )
    count = PAD // 2
    for side, target in ((core_ref[0], keep_ref), (1 - core_ref[0], send_ref)):
        span = pl.ds(pl.multiple_of(side * count, 64), count)
        target[...] = grad_ref[span].astype(target.dtype)


def shape(dtype, *dims):
    return jax.ShapeDtypeStruct(dims, dtype)


def local(
    hidden_in,
    segment_ids,
    attn_gain,
    w_query,
    b_query,
    w_key,
    b_key,
    w_value,
    b_value,
    w_out,
    ffn_gain,
    w_gate,
    w_up,
    w_down,
    cotangent,
):
    g = lax.axis_index(GROUP)
    c = lax.axis_index("c")
    rows, width = hidden_in.shape[1:]
    part = w_query.shape[1]
    units = w_down.shape[1]
    kv = w_key.shape[2]
    heads = width // HEAD_DIM

    lanes = width + 2 * kv
    k16 = kv // N
    core, group = c.reshape(1), g.reshape(1)

    def spread_out(vector):
        place = jnp.arange(N * vector.shape[0]) // vector.shape[0] == g
        return jnp.where(place, jnp.tile(vector, N), BF(0))

    bias = [spread_out(b[0]) for b in (b_query, b_key, b_value)]
    blank = jnp.zeros((2 * kv,), BF)
    small = jnp.stack(
        [
            jnp.concatenate([spread_out(attn_gain[0]), blank]),
            jnp.concatenate(bias),
            jnp.concatenate([spread_out(ffn_gain[0]), blank]),
        ]
    )
    small = jnp.pad(small, ((0, 13), (0, 0)))
    z, xh = lax.axis_index("z"), lax.axis_index("xh")
    place = jnp.stack([c, z, xh]).astype(jnp.int32)
    halves = call(
        pack_weights,
        shape(BF, N, HALF, lanes + SIDE),
        place,
        w_query[0],
        w_key[0],
        w_value[0],
        small,
        w_gate[0],
        w_up[0],
        scalars=1,
    )
    own_half = exchange(halves, GROUP)
    own_half, w_out, cotangent = lax.optimization_barrier((own_half, w_out, cotangent))
    other_half = shift(own_half, "c", 1, 2)
    group_down = lax.all_gather(cotangent[0], GROUP, axis=0, tiled=True).reshape(N, rows, width)
    out_half = to_all(at(w_out[0].reshape(2, part // 2, width), c), GROUP)
    other_half = shift(own_half, "c", 1, 2)

    segments = segment_ids[0]
    length = segments.shape[0]
    own_segments = lax.dynamic_slice_in_dim(segments, g * rows, rows, 0)
    query_index = g * rows + jnp.arange(rows, dtype=jnp.int32)
    earlier = jnp.sum((segments[None, :] < own_segments[:, None]).astype(jnp.int32), axis=-1)
    positions = query_index - earlier
    half = HEAD_DIM // 2
    frequency = THETA ** (-(2.0 * jnp.arange(half, dtype=F32)) / HEAD_DIM)
    angles = positions.astype(F32)[None, :] * frequency[:, None]
    cosine, sine = jnp.cos(angles), jnp.sin(angles)
    key_segments, own_segments = segments[:, None], own_segments[None]

    w_qkv, gains, queries, own_kv, normed, first_scale = call(
        project_tokens,
        (
            shape(BF, width, lanes),
            shape(F32, 16, lanes),
            shape(BF, width, rows),
            shape(BF, rows, 2 * kv),
            shape(BF, rows, width),
            shape(F32, rows, 1),
        ),
        core,
        hidden_in[0],
        own_half,
        other_half,
        cosine,
        sine,
        scalars=1,
    )
    second_gain = gains[2, :width]
    out_half, own_kv = lax.optimization_barrier((out_half, own_kv))
    all_kv = to_all(own_kv, GROUP).reshape(length, 2 * kv)

    out_weight = jnp.stack(core_pair(out_half, c), axis=1).reshape(width, width)
    piece = own_half[:, :, lanes:]
    pieces = jnp.stack([shift(piece, "z", -k, 4) for k in (1, 2, 3)])
    w_gu = call(
        join_units,
        shape(BF, width, 2 * PAD),
        place,
        own_half,
        other_half,
        pieces,
        shift(pieces, "c", 1, 2),
        scalars=1,
    )
    w_dn = jnp.pad(w_down[0], ((0, PAD - units), (0, 0)))

    wide = heads // KV_HEADS * rows
    attended, logsum = call(
        attend_kernel,
        (shape(BF, width, rows), shape(F32, KV_HEADS, wide)),
        group,
        queries,
        all_kv,
        key_segments,
        own_segments,
        scalars=1,
        scratch=[((length, wide), F32)],
    )
    stream = hidden_in[0].astype(F32)
    middle = stream + outer(attended, out_weight)

    second_normed, second_scale = norm_forward(middle, second_gain)
    second_normed = second_normed.astype(BF)
    inputs, hiddens, grads, seconds, downs = [], [], [], [], []
    pieces = [second_normed[:HALF], second_normed[HALF:]]
    for half in range(2):
        gathered = to_all(pieces[half], GROUP)
        second, down, hidden, grad = call(
            functools.partial(feed_forward, half),
            (
                shape(BF, N, HALF, width),
                shape(BF, N, HALF, width),
                shape(BF, N * HALF, PAD),
                shape(BF, N * HALF, 2 * PAD),
            ),
            gathered,
            group_down,
            w_gu,
            w_dn,
            flops=12 * N * HALF * width * PAD,
        )
        inputs.append(gathered)
        hiddens.append(hidden)
        grads.append(grad)
        seconds.append(second)
        downs.append(down)
    first_return = exchange(seconds[0], GROUP)
    second_return = exchange(seconds[1], GROUP)
    first_return, grads, hiddens = lax.optimization_barrier((first_return, grads, hiddens))

    cost = 4 * length * width * PAD
    unit_keep, unit_send = call(
        unit_weight_grads,
        (shape(F32, width, PAD), shape(BF, width, PAD)),
        core,
        *inputs,
        *grads,
        scalars=1,
        flops=cost,
    )
    down_keep, down_send = call(
        down_weight_grads,
        (shape(F32, PAD // 2, width), shape(BF, PAD // 2, width)),
        core,
        *hiddens,
        group_down,
        scalars=1,
        scratch=[((PAD, width), F32)],
        flops=cost // 2,
    )
    down_terms = jnp.concatenate(downs, axis=1)
    second_return, unit_send, down_send, down_terms = lax.optimization_barrier(
        (second_return, unit_send, down_send, down_terms)
    )
    grad_second = jnp.concatenate(
        [jnp.sum(part_sum.astype(F32), axis=0) for part_sum in (first_return, second_return)]
    )
    unit_share = (unit_keep + shift(unit_send, "c", 1, 2).astype(F32)).astype(BF)
    down_share = (down_keep + shift(down_send, "c", 1, 2).astype(F32)).astype(BF)
    blocks = unit_share.reshape(N, part // 16, 16, PAD)
    blocks = jnp.pad(blocks, ((0, 0), (0, N - part // 16), (0, 0), (0, 0)))
    blocks = jnp.moveaxis(blocks, 1, 0).reshape(2, 4, N, 16, PAD)

    def along_z(k):
        return lax.dynamic_index_in_dim(blocks, (z + k) % 4, 1, keepdims=False)

    unit_share = along_z(0).astype(F32)
    for k in (1, 3, 2):
        unit_share = unit_share + shift(along_z(k), "z", k, 4).astype(F32)

    down_arrived = exchange(down_terms, GROUP)

    stream_grad = cotangent[0].astype(F32)
    term, gain_second = norm_backward(middle, second_scale, second_gain, grad_second)
    grad_middle = stream_grad + term
    attn_grad = grad_middle.astype(BF)
    grad_attended = mm_t(out_weight, attn_grad).astype(BF)
    small = jnp.pad(gain_second.reshape(N, 1, part), ((0, 0), (0, 15), (0, width - part)))
    grad_out = mm(attended, attn_grad).reshape(N, part, width)
    grad_out = jnp.concatenate([grad_out, small], axis=1)
    out_share = core_sum(grad_out[:, :HALF], grad_out[:, HALF:], c)
    grad_q, grad_kv = call(
        attend_back_kernel,
        (shape(BF, rows, width), shape(BF, length, 2 * kv)),
        group,
        queries,
        all_kv,
        key_segments,
        own_segments,
        grad_attended,
        logsum,
        cosine,
        sine,
        scalars=1,
        scratch=[((length, wide), F32)] * 2,
    )
    grad_kv, down_arrived = lax.optimization_barrier((grad_kv, down_arrived))
    arrived = exchange(grad_kv.reshape(N, rows, 2 * kv), GROUP)

    arrived, out_share, unit_share = lax.optimization_barrier((arrived, out_share, unit_share))

    sent = shift(at(unit_share, 1 - xh).astype(BF), "xh", 1, 2)
    unit_share = (at(unit_share, xh) + sent.astype(F32)).astype(BF)
    tiles = [unit_share[:, :, 128 * t : 128 * (t + 1)] for t in range(5)]
    tiles += [jnp.zeros_like(tiles[0])] * 3
    tiles = [jnp.concatenate(tiles[2 * i : 2 * i + 2], axis=2) for i in range(4)]
    unit_share = jnp.concatenate(tiles, axis=1)

    grad_in, keep, send = call(
        tail_kernel,
        (shape(F32, rows, width), shape(F32, N, HALF, lanes), shape(BF, N, HALF, lanes)),
        core,
        arrived,
        grad_q,
        w_qkv,
        hidden_in[0],
        first_scale,
        gains,
        normed,
        grad_middle,
        cosine,
        sine,
        scalars=1,
        scratch=[((rows, lanes), BF), ((width, lanes), F32), ((8, lanes), F32), ((N, 16, lanes), F32)],
    )
    grad_in = grad_in[None]
    share = (keep + shift(send, "c", 1, 2).astype(F32)).astype(BF)
    share, unit_share, down_arrived = lax.optimization_barrier((share, unit_share, down_arrived))
    arrived = exchange(jnp.concatenate([share, out_share, unit_share], axis=2), GROUP)
    layer_out = middle + jnp.sum(down_arrived.astype(F32), axis=0)
    hidden_out = layer_out.astype(BF)[None]
    share, columns = call(
        pack_last,
        (shape(BF, N, HALF, width), shape(BF, N, 48, 256)),
        arrived,
        down_share,
        scratch=[((HALF, lanes + width), BF)],
    )
    columns = jnp.stack([columns, shift(columns, "xh", 1, 2)])
    columns = jnp.stack([columns] + [shift(columns, "z", -k, 4) for k in (1, 2, 3)])

    share = to_all(sum_at(share, SPREAD).astype(BF), SPREAD)
    other_columns = shift(columns, "c", 1, 2)
    share, other_columns = lax.optimization_barrier((share, other_columns))
    other_share = shift(share, "c", 1, 2)
    units_out = (shape(F32, part, N * units),) * 2
    units_out = call(
        unpack_units, units_out, place, columns, other_columns, scalars=1
    )
    grad_w_gate, grad_w_up = [grad[None] for grad in units_out]
    narrow = [shape(F32, 1, count) for count in (part, k16, k16, part, part)]
    down, w_q, w_k, w_v, w_o, b_q, b_k, b_v, first, second = call(
        unpack_last,
        (
            shape(F32, units, width),
            shape(F32, part, width),
            shape(F32, part, kv),
            shape(F32, part, kv),
            shape(F32, part, width),
            *narrow,
        ),
        core,
        share,
        other_share,
        scalars=1,
    )
    weights = (first, w_q[None], b_q, w_k[None], b_k, w_v[None], b_v, w_o[None], second)
    return (hidden_out, grad_in) + weights + (grad_w_gate, grad_w_up, down[None])


def solution(mesh):
    split = Mesh(mesh.devices.reshape(SIZES), AXES)
    tokens = P(REPLICA, GROUP, None)
    vector = P(None, GROUP)
    matrix = P(None, GROUP, None)
    weights = (vector, matrix, vector, matrix, vector, matrix, vector, matrix, vector)
    return jax.shard_map(
        local,
        mesh=split,
        in_specs=(tokens, P(REPLICA, None)) + weights + (matrix,) * 3 + (tokens,),
        out_specs=(tokens, tokens) + weights + (matrix,) * 3,
        check_vma=False,
    )
```

```python
import functools

import jax
import jax.numpy as jnp
from jax import lax
from jax.experimental import pallas as pl
from jax.experimental.pallas import tpu as pltpu
from jax.sharding import Mesh
from jax.sharding import PartitionSpec as P

KV_HEADS = 2
HEAD_DIM = 64
EPS = 1e-06
THETA = 1000000.0
MASKED_SCORE = -1e30
GROUP = ("y", "xl")
SPREAD = ("xh", "z")
REPLICA = ("xh", "z", "c")
SIZES = (4, 2, 2, 4, 2)
AXES = ("y", "xl", "xh", "z", "c")
N = 8
PAD = 640
HALF = 64
BF = jnp.bfloat16
F32 = jnp.float32


def shift(array, axis, by, size):
    return lax.ppermute(array, axis, [(i, (i + by) % size) for i in range(size)])


def exchange(blocks, axis):
    return lax.all_to_all(blocks, axis, 0, 0, tiled=True)


def to_all(array, axis):
    return exchange(jnp.broadcast_to(array, (N, *array.shape)), axis)


def sum_at(blocks, axis):
    return jnp.sum(exchange(blocks, axis).astype(F32), axis=0)


def at(blocks, index):
    return lax.dynamic_index_in_dim(blocks, index, 0, keepdims=False)


def norm_forward(stream, gain):
    scale = lax.rsqrt(jnp.mean(stream * stream, axis=-1, keepdims=True) + EPS)
    return stream * scale * gain, scale


def norm_backward(stream, scale, gain, gradient):
    normalized = stream * scale
    scaled = gradient * gain
    gain_grad = jnp.sum(gradient * normalized, axis=0)
    grad = scale * (scaled - normalized * jnp.mean(scaled * normalized, axis=-1, keepdims=True))
    return grad, gain_grad


def mm(a, b):
    return jnp.dot(a, b, preferred_element_type=F32)


def mm_t(a, b):
    return lax.dot_general(a, b, (((1,), (1,)), ((), ())), preferred_element_type=F32)


def outer(a, b):
    return lax.dot_general(a, b, (((0,), (0,)), ((), ())), preferred_element_type=F32)


def core_sum(first, second, c):
    low = c == 0
    keep = jnp.where(low, first, second)
    send = jnp.where(low, second, first).astype(BF)
    return (keep + shift(send, "c", 1, 2).astype(F32)).astype(BF)


def core_pair(own, c):
    other = shift(own, "c", 1, 2)
    low = c == 0
    return jnp.where(low, own, other), jnp.where(low, other, own)


def unpack_units(place_ref, own_ref, other_ref, gate_ref, up_ref):
    units = gate_ref.shape[1] // N
    c, z, xh = place_ref[0], place_ref[1], place_ref[2]

    def write(source, target):
        for piece in range(target.shape[0] // 16):
            slot = lax.rem(piece % 4 + 4 - z, 4)
            second = lax.rem(xh + piece // 4, 2)
            for j in range(N):
                for t in range(5):
                    count = min(128, units - 128 * t)
                    row, lane = 16 * (t // 2), 128 * (t % 2)
                    tile = source[slot, second, j, row : row + 16, lane : lane + count]
                    start = units * j + 128 * t
                    target[16 * piece : 16 * piece + 16, start : start + count] = tile.astype(F32)

    @pl.when(c == 0)
    def _():
        write(own_ref, gate_ref)
        write(other_ref, up_ref)

    @pl.when(c != 0)
    def _():
        write(other_ref, gate_ref)
        write(own_ref, up_ref)


VMEM = pl.BlockSpec(memory_space=pltpu.VMEM)
SMEM = pl.BlockSpec(memory_space=pltpu.SMEM)


def call(kernel, outs, *args, scalars=0, scratch=(), flops=0, mib=48):
    cost = pl.CostEstimate(flops=flops, bytes_accessed=2**20, transcendentals=0)
    return pl.pallas_call(
        kernel,
        out_shape=outs,
        in_specs=[SMEM] * scalars + [VMEM] * (len(args) - scalars),
        out_specs=jax.tree.map(lambda _: VMEM, outs),
        scratch_shapes=[pltpu.VMEM(shape, dtype) for shape, dtype in scratch],
        compiler_params=pltpu.CompilerParams(vmem_limit_bytes=mib * 2**20),
        cost_estimate=cost,
    )(*args)


SIDE = 384


def pack_weights(place_ref, q_ref, k_ref, v_ref, row_ref, gate_ref, up_ref, out_ref):
    part = q_ref.shape[0]
    width, kv = q_ref.shape[1], k_ref.shape[1]
    lanes = width + 2 * kv
    units = gate_ref.shape[1] // N
    spans = ((0, q_ref), (width, k_ref), (width + kv, v_ref))
    out_ref[:, :, lanes:] = jnp.zeros((N, HALF, SIDE), BF)
    first = pl.multiple_of(piece_start(place_ref[1], part), 16)

    def beside(ref):
        for j in range(N):
            for t in range(5):
                count = min(128, units - 128 * t)
                start = units * j + 128 * t
                row, lane = 32 * (t // 3), lanes + 128 * (t % 3)
                tile = ref[pl.ds(first, 32), start : start + count]
                out_ref[j, row : row + 32, lane : lane + count] = tile

    @pl.when(place_ref[0] == 0)
    def _():
        beside(gate_ref)
        for j in range(N):
            for start, ref in spans:
                out_ref[j, :, start : start + ref.shape[1]] = ref[:HALF]

    @pl.when(place_ref[0] != 0)
    def _():
        beside(up_ref)
        for j in range(N):
            for start, ref in spans:
                out_ref[j, : part - HALF, start : start + ref.shape[1]] = ref[HALF:]
            out_ref[j, part - HALF :, :lanes] = row_ref[...]


def piece_start(z, part):
    return jnp.minimum(32 * z, part - 32)


def join_units(place_ref, own_ref, other_ref, own_z_ref, other_z_ref, w_ref):
    part = w_ref.shape[0] // N
    lanes = own_ref.shape[2] - SIDE
    z = place_ref[1]

    def write(sources, side):
        near, far = sources

        @pl.loop(0, N)
        def _(j):
            for k in range(4):
                start = part * j + piece_start(lax.rem(z + k, 4), part)
                rows = pl.ds(pl.multiple_of(start, 16), 32)
                for t in range(5):
                    row, lane = 32 * (t // 3), 128 * (t % 3)
                    if k == 0:
                        tile = near[j, row : row + 32, lanes + lane : lanes + lane + 128]
                    else:
                        tile = far[k - 1, j, row : row + 32, lane : lane + 128]
                    column = side * PAD + 128 * t
                    w_ref[rows, column : column + 128] = tile

    @pl.when(place_ref[0] == 0)
    def _():
        write((own_ref, own_z_ref), 0)
        write((other_ref, other_z_ref), 1)

    @pl.when(place_ref[0] != 0)
    def _():
        write((own_ref, own_z_ref), 1)
        write((other_ref, other_z_ref), 0)


def dot(a, b, da, db):
    return lax.dot_general(a, b, (((da,), (db,)), ((), ())), preferred_element_type=F32)


def turned_rows(block, cos, sin, back):
    half = HEAD_DIM // 2
    top, low = block[:half], block[half:]
    if back:
        return [top * cos + low * sin, low * cos - top * sin]
    return [top * cos - low * sin, low * cos + top * sin]


def project_tokens(core_ref, x_ref, own_ref, other_ref, cos_ref, sin_ref, w_ref, rows_ref, q_ref, kv_ref, n_ref, scale_ref):
    part = w_ref.shape[0] // N
    width = x_ref.shape[1]
    lanes = w_ref.shape[1]
    kv = (lanes - width) // 2

    def assemble(low, high):
        small = jnp.zeros((16, lanes), F32)
        for j in range(N):
            w_ref[part * j : part * j + HALF] = low[j, :, :lanes]
            w_ref[part * j + HALF : part * (j + 1)] = high[j, : part - HALF, :lanes]
            small = small + high[j, part - HALF :, :lanes].astype(F32)
        rows_ref[...] = small

    @pl.when(core_ref[0] == 0)
    def _():
        assemble(own_ref, other_ref)

    @pl.when(core_ref[0] != 0)
    def _():
        assemble(other_ref, own_ref)

    x = x_ref[...].astype(F32)
    scale = lax.rsqrt(jnp.mean(x * x, axis=-1, keepdims=True) + EPS)
    scale_ref[...] = scale
    normed = (x * scale * rows_ref[0:1, :width]).astype(BF)
    n_ref[...] = normed
    raw = dot(normed, w_ref[...], 1, 0) + rows_ref[1:2, :]
    kv_ref[:, kv:] = raw[:, width + kv :].astype(BF)
    turned = raw[:, : width + kv].T
    cos, sin = cos_ref[...], sin_ref[...]
    for h in range(width // HEAD_DIM):
        block = turned[h * HEAD_DIM : (h + 1) * HEAD_DIM]
        q_ref[h * HEAD_DIM : (h + 1) * HEAD_DIM] = jnp.concatenate(
            turned_rows(block, cos, sin, False)
        ).astype(BF)
    keys = []
    for h in range(width // HEAD_DIM, (width + kv) // HEAD_DIM):
        keys += turned_rows(turned[h * HEAD_DIM : (h + 1) * HEAD_DIM], cos, sin, False)
    kv_ref[:, :kv] = jnp.concatenate(keys).T.astype(BF)


CHUNK = 256


def heads_side_by_side(ref, first, ratio):
    return jnp.concatenate(
        [ref[(first + i) * HEAD_DIM : (first + i + 1) * HEAD_DIM] for i in range(ratio)], axis=1
    )


def mask_bias(start, group, key_ref, own_ref, rows, ratio):
    key = start + lax.broadcasted_iota(jnp.int32, (CHUNK, rows), 0)
    query = group * rows + lax.broadcasted_iota(jnp.int32, (CHUNK, rows), 1)
    allowed = (key <= query) & (key_ref[start : start + CHUNK] == own_ref[...])
    bias = jnp.where(allowed, 0.0, MASKED_SCORE)
    return jnp.concatenate([bias] * ratio, axis=1)


def attend_kernel(group_ref, q_ref, kv_ref, key_ref, own_ref, out_ref, log_ref, score_ref):
    rows = q_ref.shape[1]
    length = kv_ref.shape[0]
    kv = kv_ref.shape[1] // 2
    ratio = q_ref.shape[0] // kv
    starts = range(0, length, CHUNK)
    for head in range(KV_HEADS):
        queries = heads_side_by_side(q_ref, head * ratio, ratio) * BF(HEAD_DIM**-0.5)
        span = slice(head * HEAD_DIM, (head + 1) * HEAD_DIM)
        top = jnp.full((1, ratio * rows), MASKED_SCORE, F32)
        for start in starts:
            scores = dot(kv_ref[start : start + CHUNK, span], queries, 1, 0)
            scores = scores + mask_bias(start, group_ref[0], key_ref, own_ref, rows, ratio)
            score_ref[start : start + CHUNK] = scores
            top = jnp.maximum(top, jnp.max(scores, axis=0, keepdims=True))
        total = jnp.zeros_like(top)
        mixed = jnp.zeros((HEAD_DIM, ratio * rows), F32)
        for start in starts:
            weights = jnp.exp(score_ref[start : start + CHUNK] - top)
            total = total + jnp.sum(weights, axis=0, keepdims=True)
            values = kv_ref[start : start + CHUNK, kv:][:, span]
            mixed = mixed + dot(values, weights.astype(BF), 0, 0)
        log_ref[head : head + 1] = top + jnp.log(total)
        mixed = (mixed / total).astype(BF)
        for i in range(ratio):
            at_head = (head * ratio + i) * HEAD_DIM
            out_ref[at_head : at_head + HEAD_DIM] = mixed[:, i * rows : (i + 1) * rows]


def attend_back_kernel(group_ref, q_ref, kv_ref, key_ref, own_ref, grad_ref, log_ref, cos_ref, sin_ref, gq_ref, gkv_ref, prob_ref, diff_ref):
    rows = q_ref.shape[1]
    length = kv_ref.shape[0]
    kv = kv_ref.shape[1] // 2
    ratio = q_ref.shape[0] // kv
    starts = range(0, length, CHUNK)
    cos, sin = cos_ref[...], sin_ref[...]
    grads_k, grads_v = [[], []], [[], []]
    for head in range(KV_HEADS):
        queries = heads_side_by_side(q_ref, head * ratio, ratio) * BF(HEAD_DIM**-0.5)
        grads = heads_side_by_side(grad_ref, head * ratio, ratio)
        span = slice(head * HEAD_DIM, (head + 1) * HEAD_DIM)
        log = log_ref[head : head + 1]
        inner = jnp.zeros((1, ratio * rows), F32)
        for start in starts:
            scores = dot(kv_ref[start : start + CHUNK, span], queries, 1, 0)
            scores = scores + mask_bias(start, group_ref[0], key_ref, own_ref, rows, ratio)
            probs = jnp.exp(scores - log)
            prob_ref[start : start + CHUNK] = probs
            diff = dot(kv_ref[start : start + CHUNK, kv:][:, span], grads, 1, 0)
            diff_ref[start : start + CHUNK] = diff
            inner = inner + jnp.sum(probs * diff, axis=0, keepdims=True)
        grad_q = jnp.zeros((HEAD_DIM, ratio * rows), F32)
        for start in starts:
            probs = prob_ref[start : start + CHUNK]
            grad_s = (probs * (diff_ref[start : start + CHUNK] - inner)).astype(BF)
            grads_k[head].append(dot(grad_s, queries, 1, 1))
            grads_v[head].append(dot(probs.astype(BF), grads, 1, 1))
            grad_q = grad_q + dot(kv_ref[start : start + CHUNK, span], grad_s, 0, 0)
        grad_q = grad_q * HEAD_DIM**-0.5
        blocks = []
        for i in range(ratio):
            blocks += turned_rows(grad_q[:, i * rows : (i + 1) * rows], cos, sin, True)
        lanes = ratio * HEAD_DIM
        gq_ref[:, head * lanes : (head + 1) * lanes] = jnp.concatenate(blocks).T.astype(BF)
    for i, start in enumerate(starts):
        parts = [grads_k[0][i], grads_k[1][i], grads_v[0][i], grads_v[1][i]]
        gkv_ref[start : start + CHUNK] = jnp.concatenate(parts, axis=1).astype(BF)


def join_shares(keep_ref, sent_ref, out_share_ref, unit_ref, joined_ref):
    lanes, width = keep_ref.shape[2], out_share_ref.shape[2]
    joined_ref[:, :, :lanes] = (keep_ref[...] + sent_ref[...].astype(F32)).astype(BF)
    joined_ref[:, :, lanes : lanes + width] = out_share_ref[...]
    joined_ref[:, :, lanes + width :] = unit_ref[...]


def tail_kernel(core_ref, arrived_ref, gq_ref, w_ref, x_ref, scale_ref, rows_ref, n_ref, mid_ref, cos_ref, sin_ref, in_ref, keep_ref, send_ref, g_ref, share_ref, line_ref, small_ref):
    rows, width = x_ref.shape
    lanes = w_ref.shape[1]
    kv = (lanes - width) // 2
    part = width // N
    total = arrived_ref[0].astype(F32)
    for j in range(1, N):
        total = total + arrived_ref[j].astype(F32)
    turned = total[:, :kv].T
    keys = []
    for h in range(KV_HEADS):
        block = turned[h * HEAD_DIM : (h + 1) * HEAD_DIM]
        keys += turned_rows(block, cos_ref[...], sin_ref[...], True)
    g_ref[:, :width] = gq_ref[...]
    g_ref[:, width : width + kv] = jnp.concatenate(keys).T.astype(BF)
    g_ref[:, width + kv :] = total[:, kv:].astype(BF)
    grads = g_ref[...]
    first = dot(grads, w_ref[...], 1, 1)
    scale = scale_ref[...]
    normalized = x_ref[...].astype(F32) * scale
    scaled = first * rows_ref[0:1, :width]
    mean = jnp.mean(scaled * normalized, axis=-1, keepdims=True)
    in_ref[...] = mid_ref[...] + scale * (scaled - normalized * mean)
    gain = jnp.sum(first * normalized, axis=0, keepdims=True)
    share_ref[...] = dot(n_ref[...], grads, 0, 0)
    bias = jnp.sum(grads.astype(F32), axis=0, keepdims=True)
    line_ref[0:1] = bias
    line_ref[1:2, :width] = gain
    small_ref[...] = jnp.zeros_like(small_ref)
    narrow = kv // N
    for j in range(N):
        at_lane = 0
        for row, start, count in (
            (0, part * j, part),
            (0, width + narrow * j, narrow),
            (0, width + kv + narrow * j, narrow),
            (1, part * j, part),
        ):
            piece = line_ref[row : row + 1, start : start + count]
            small_ref[j, 0:1, at_lane : at_lane + count] = piece
            at_lane += count

    def write(low, high):
        for j in range(N):
            low[j] = share_ref[part * j : part * j + HALF].astype(low.dtype)
            high[j, : part - HALF] = share_ref[part * j + HALF : part * (j + 1)].astype(high.dtype)
            high[j, part - HALF :] = small_ref[j].astype(high.dtype)

    @pl.when(core_ref[0] == 0)
    def _():
        write(keep_ref, send_ref)

    @pl.when(core_ref[0] != 0)
    def _():
        write(send_ref, keep_ref)


def pack_last(arrived_ref, down_ref, out_ref, columns_ref, sum_ref):
    width = out_ref.shape[2]
    lanes = sum_ref.shape[1] - width
    total = arrived_ref[0, :, : lanes + width].astype(F32)
    for j in range(1, N):
        total = total + arrived_ref[j, :, : lanes + width].astype(F32)
    sum_ref[...] = total.astype(BF)
    columns_ref[...] = arrived_ref[:, :48, lanes + width :]
    for p in range(6):
        out_ref[p, :48] = down_ref[48 * p : 48 * p + 48]
    out_ref[6, :32] = down_ref[288:320]
    out_ref[6, 32:48] = sum_ref[:16, lanes:]
    out_ref[7, :48] = sum_ref[16:HALF, lanes:]
    out_ref[:, 48:] = jnp.zeros((N, 16, width), BF)
    across = lanes // 128
    for i in range(4 * across):
        r, l = i // across, i % across
        tile = sum_ref[16 * r : 16 * r + 16, 128 * l : 128 * l + 128]
        out_ref[i // 5, 48:HALF, 128 * (i % 5) : 128 * (i % 5) + 128] = tile


def unpack_last(core_ref, own_ref, other_ref, down_ref, q_ref, k_ref, v_ref, out_ref, bq_ref, bk_ref, bv_ref, first_ref, second_ref):
    part, narrow = bq_ref.shape[1], bk_ref.shape[1]
    across = q_ref.shape[1] // 128 + 2

    def write(source, half):
        for p in range(6):
            start = 320 * half + 48 * p
            down_ref[start : start + 48] = source[p, :48].astype(F32)
        if half == 0:
            down_ref[288:320] = source[6, :32].astype(F32)
        first = HALF * half
        out_ref[first : first + 16] = source[6, 32:48].astype(F32)
        count = 48 - 16 * half
        out_ref[first + 16 : first + 16 + count] = source[7, :count].astype(F32)
        if half == 1:
            second_ref[...] = source[7, 32:48].astype(F32)[:1, :part]
        for i in range((4 - half) * across):
            r, l = i // across, i % across
            tile = source[i // 5, 48:HALF, 128 * (i % 5) : 128 * (i % 5) + 128].astype(F32)
            rows = slice(first + 16 * r, first + 16 * r + 16)
            if l < across - 2:
                q_ref[rows, 128 * l : 128 * l + 128] = tile
            elif l == across - 2:
                k_ref[rows] = tile
            else:
                v_ref[rows] = tile
        if half == 1:
            i = 3 * across
            line = [source[n // 5, 48:HALF, 128 * (n % 5) : 128 * (n % 5) + 128] for n in (i, i + 1)]
            line = jnp.concatenate(line, axis=1).astype(F32)[:1]
            bq_ref[...] = line[:, :part]
            bk_ref[...] = line[:, part : part + narrow]
            bv_ref[...] = line[:, part + narrow : part + 2 * narrow]
            first_ref[...] = line[:, part + 2 * narrow : 2 * part + 2 * narrow]

    @pl.when(core_ref[0] == 0)
    def _():
        write(own_ref, 0)
        write(other_ref, 1)

    @pl.when(core_ref[0] != 0)
    def _():
        write(other_ref, 0)
        write(own_ref, 1)


def halves_of(ref, half):
    block = ref[:, half * HALF : (half + 1) * HALF]
    return block.reshape(-1, ref.shape[2])


def feed_forward(half, x_ref, cot_ref, gu_ref, dn_ref, second_ref, down_ref, hidden_ref, grad_ref):
    step = 4
    for at_block in range(0, N, step):
        x = x_ref[at_block : at_block + step].reshape(step * HALF, -1)
        cot = cot_ref[at_block : at_block + step, half * HALF : (half + 1) * HALF]
        cot = cot.reshape(step * HALF, -1)
        gate = dot(x, gu_ref[:, :PAD], 1, 0)
        up = dot(x, gu_ref[:, PAD:], 1, 0)
        back = dot(cot, dn_ref[...], 1, 1)
        sigmoid = jax.nn.sigmoid(gate)
        silu = gate * sigmoid
        hidden = (silu * up).astype(BF)
        grad_gate = (back * up * sigmoid * (1.0 + gate * (1.0 - sigmoid))).astype(BF)
        grad_up = (back * silu).astype(BF)
        span = slice(at_block * HALF, (at_block + step) * HALF)
        hidden_ref[span] = hidden
        grad_ref[span, :PAD] = grad_gate
        grad_ref[span, PAD:] = grad_up
        second = dot(grad_gate, gu_ref[:, :PAD], 1, 1) + dot(grad_up, gu_ref[:, PAD:], 1, 1)
        second_ref[at_block : at_block + step] = second.astype(BF).reshape(step, HALF, -1)
        down = dot(hidden, dn_ref[...], 1, 0)
        down_ref[at_block : at_block + step] = down.astype(BF).reshape(step, HALF, -1)


def unit_weight_grads(core_ref, xa_ref, xb_ref, ga_ref, gb_ref, keep_ref, send_ref):
    xa, xb = xa_ref[...].reshape(N * HALF, -1), xb_ref[...].reshape(N * HALF, -1)
    for side, target in ((core_ref[0], keep_ref), (1 - core_ref[0], send_ref)):
        span = pl.ds(pl.multiple_of(side * PAD, 128), PAD)
        grad = dot(xa, ga_ref[:, span], 0, 0) + dot(xb, gb_ref[:, span], 0, 0)
        target[...] = grad.astype(target.dtype)


def down_weight_grads(core_ref, ha_ref, hb_ref, cot_ref, keep_ref, send_ref, grad_ref):
    grad_ref[...] = dot(ha_ref[...], halves_of(cot_ref, 0), 0, 0) + dot(
        hb_ref[...], halves_of(cot_ref, 1), 0, 0
    )
    count = PAD // 2
    for side, target in ((core_ref[0], keep_ref), (1 - core_ref[0], send_ref)):
        span = pl.ds(pl.multiple_of(side * count, 64), count)
        target[...] = grad_ref[span].astype(target.dtype)


def shape(dtype, *dims):
    return jax.ShapeDtypeStruct(dims, dtype)


def local(
    hidden_in,
    segment_ids,
    attn_gain,
    w_query,
    b_query,
    w_key,
    b_key,
    w_value,
    b_value,
    w_out,
    ffn_gain,
    w_gate,
    w_up,
    w_down,
    cotangent,
):
    g = lax.axis_index(GROUP)
    c = lax.axis_index("c")
    rows, width = hidden_in.shape[1:]
    part = w_query.shape[1]
    units = w_down.shape[1]
    kv = w_key.shape[2]
    heads = width // HEAD_DIM

    lanes = width + 2 * kv
    k16 = kv // N
    core, group = c.reshape(1), g.reshape(1)

    def spread_out(vector):
        place = jnp.arange(N * vector.shape[0]) // vector.shape[0] == g
        return jnp.where(place, jnp.tile(vector, N), BF(0))

    bias = [spread_out(b[0]) for b in (b_query, b_key, b_value)]
    blank = jnp.zeros((2 * kv,), BF)
    small = jnp.stack(
        [
            jnp.concatenate([spread_out(attn_gain[0]), blank]),
            jnp.concatenate(bias),
            jnp.concatenate([spread_out(ffn_gain[0]), blank]),
        ]
    )
    small = jnp.pad(small, ((0, 13), (0, 0)))
    z, xh = lax.axis_index("z"), lax.axis_index("xh")
    place = jnp.stack([c, z, xh]).astype(jnp.int32)
    halves = call(
        pack_weights,
        shape(BF, N, HALF, lanes + SIDE),
        place,
        w_query[0],
        w_key[0],
        w_value[0],
        small,
        w_gate[0],
        w_up[0],
        scalars=1,
    )
    own_half = exchange(halves, GROUP)
    own_half, w_out, cotangent = lax.optimization_barrier((own_half, w_out, cotangent))
    other_half = shift(own_half, "c", 1, 2)
    group_down = lax.all_gather(cotangent[0], GROUP, axis=0, tiled=True).reshape(N, rows, width)
    out_half = to_all(at(w_out[0].reshape(2, part // 2, width), c), GROUP)
    other_half = shift(own_half, "c", 1, 2)

    segments = segment_ids[0]
    length = segments.shape[0]
    own_segments = lax.dynamic_slice_in_dim(segments, g * rows, rows, 0)
    query_index = g * rows + jnp.arange(rows, dtype=jnp.int32)
    earlier = jnp.sum((segments[None, :] < own_segments[:, None]).astype(jnp.int32), axis=-1)
    positions = query_index - earlier
    half = HEAD_DIM // 2
    frequency = THETA ** (-(2.0 * jnp.arange(half, dtype=F32)) / HEAD_DIM)
    angles = positions.astype(F32)[None, :] * frequency[:, None]
    cosine, sine = jnp.cos(angles), jnp.sin(angles)
    key_segments, own_segments = segments[:, None], own_segments[None]

    w_qkv, gains, queries, own_kv, normed, first_scale = call(
        project_tokens,
        (
            shape(BF, width, lanes),
            shape(F32, 16, lanes),
            shape(BF, width, rows),
            shape(BF, rows, 2 * kv),
            shape(BF, rows, width),
            shape(F32, rows, 1),
        ),
        core,
        hidden_in[0],
        own_half,
        other_half,
        cosine,
        sine,
        scalars=1,
    )
    second_gain = gains[2, :width]
    w_dn = jnp.pad(w_down[0], ((0, PAD - units), (0, 0)))
    out_half, own_kv, w_dn = lax.optimization_barrier((out_half, own_kv, w_dn))
    all_kv = to_all(own_kv, GROUP).reshape(length, 2 * kv)

    out_weight = jnp.stack(core_pair(out_half, c), axis=1).reshape(width, width)
    all_kv, out_weight = lax.optimization_barrier((all_kv, out_weight))
    piece = own_half[:, :, lanes:]
    pieces = jnp.stack([shift(piece, "z", -k, 4) for k in (1, 2, 3)])
    w_gu = call(
        join_units,
        shape(BF, width, 2 * PAD),
        place,
        own_half,
        other_half,
        pieces,
        shift(pieces, "c", 1, 2),
        scalars=1,
    )

    wide = heads // KV_HEADS * rows
    attended, logsum = call(
        attend_kernel,
        (shape(BF, width, rows), shape(F32, KV_HEADS, wide)),
        group,
        queries,
        all_kv,
        key_segments,
        own_segments,
        scalars=1,
        scratch=[((length, wide), F32)],
    )
    stream = hidden_in[0].astype(F32)
    middle = stream + outer(attended, out_weight)

    second_normed, second_scale = norm_forward(middle, second_gain)
    second_normed = second_normed.astype(BF)
    inputs, hiddens, grads, seconds, downs = [], [], [], [], []
    pieces = [second_normed[:HALF], second_normed[HALF:]]
    for half in range(2):
        gathered = to_all(pieces[half], GROUP)
        second, down, hidden, grad = call(
            functools.partial(feed_forward, half),
            (
                shape(BF, N, HALF, width),
                shape(BF, N, HALF, width),
                shape(BF, N * HALF, PAD),
                shape(BF, N * HALF, 2 * PAD),
            ),
            gathered,
            group_down,
            w_gu,
            w_dn,
            flops=12 * N * HALF * width * PAD,
        )
        inputs.append(gathered)
        hiddens.append(hidden)
        grads.append(grad)
        seconds.append(second)
        downs.append(down)
    first_return = exchange(seconds[0], GROUP)
    second_return = exchange(seconds[1], GROUP)
    first_return, grads, hiddens = lax.optimization_barrier((first_return, grads, hiddens))

    cost = 4 * length * width * PAD
    unit_keep, unit_send = call(
        unit_weight_grads,
        (shape(F32, width, PAD), shape(BF, width, PAD)),
        core,
        *inputs,
        *grads,
        scalars=1,
        flops=cost,
    )
    down_keep, down_send = call(
        down_weight_grads,
        (shape(F32, PAD // 2, width), shape(BF, PAD // 2, width)),
        core,
        *hiddens,
        group_down,
        scalars=1,
        scratch=[((PAD, width), F32)],
        flops=cost // 2,
    )
    down_terms = jnp.concatenate(downs, axis=1)
    second_return, unit_send, down_send, down_terms = lax.optimization_barrier(
        (second_return, unit_send, down_send, down_terms)
    )
    grad_second = jnp.concatenate(
        [jnp.sum(part_sum.astype(F32), axis=0) for part_sum in (first_return, second_return)]
    )
    unit_share = (unit_keep + shift(unit_send, "c", 1, 2).astype(F32)).astype(BF)
    down_share = (down_keep + shift(down_send, "c", 1, 2).astype(F32)).astype(BF)
    blocks = unit_share.reshape(N, part // 16, 16, PAD)
    blocks = jnp.pad(blocks, ((0, 0), (0, N - part // 16), (0, 0), (0, 0)))
    blocks = jnp.moveaxis(blocks, 1, 0).reshape(2, 4, N, 16, PAD)

    def along_z(k):
        return lax.dynamic_index_in_dim(blocks, (z + k) % 4, 1, keepdims=False)

    unit_share = along_z(0).astype(F32)
    for k in (1, 3, 2):
        unit_share = unit_share + shift(along_z(k), "z", k, 4).astype(F32)

    down_arrived = exchange(down_terms, GROUP)

    stream_grad = cotangent[0].astype(F32)
    term, gain_second = norm_backward(middle, second_scale, second_gain, grad_second)
    grad_middle = stream_grad + term
    attn_grad = grad_middle.astype(BF)
    grad_attended = mm_t(out_weight, attn_grad).astype(BF)
    small = jnp.pad(gain_second.reshape(N, 1, part), ((0, 0), (0, 15), (0, width - part)))
    grad_out = mm(attended, attn_grad).reshape(N, part, width)
    grad_out = jnp.concatenate([grad_out, small], axis=1)
    out_share = core_sum(grad_out[:, :HALF], grad_out[:, HALF:], c)
    grad_q, grad_kv = call(
        attend_back_kernel,
        (shape(BF, rows, width), shape(BF, length, 2 * kv)),
        group,
        queries,
        all_kv,
        key_segments,
        own_segments,
        grad_attended,
        logsum,
        cosine,
        sine,
        scalars=1,
        scratch=[((length, wide), F32)] * 2,
    )
    grad_kv, down_arrived = lax.optimization_barrier((grad_kv, down_arrived))
    arrived = exchange(grad_kv.reshape(N, rows, 2 * kv), GROUP)

    arrived, out_share, unit_share = lax.optimization_barrier((arrived, out_share, unit_share))

    sent = shift(at(unit_share, 1 - xh).astype(BF), "xh", 1, 2)
    unit_share = (at(unit_share, xh) + sent.astype(F32)).astype(BF)
    tiles = [unit_share[:, :, 128 * t : 128 * (t + 1)] for t in range(5)]
    tiles += [jnp.zeros_like(tiles[0])] * 3
    tiles = [jnp.concatenate(tiles[2 * i : 2 * i + 2], axis=2) for i in range(4)]
    unit_share = jnp.concatenate(tiles, axis=1)

    grad_in, keep, send = call(
        tail_kernel,
        (shape(F32, rows, width), shape(F32, N, HALF, lanes), shape(BF, N, HALF, lanes)),
        core,
        arrived,
        grad_q,
        w_qkv,
        hidden_in[0],
        first_scale,
        gains,
        normed,
        grad_middle,
        cosine,
        sine,
        scalars=1,
        scratch=[((rows, lanes), BF), ((width, lanes), F32), ((8, lanes), F32), ((N, 16, lanes), F32)],
    )
    grad_in = grad_in[None]
    share = shift(send, "c", 1, 2)
    share, unit_share, down_arrived = lax.optimization_barrier((share, unit_share, down_arrived))
    share = call(
        join_shares, shape(BF, N, HALF, lanes + width + 256), keep, share, out_share, unit_share
    )
    arrived = exchange(share, GROUP)
    layer_out = middle + jnp.sum(down_arrived.astype(F32), axis=0)
    hidden_out = layer_out.astype(BF)[None]
    share, columns = call(
        pack_last,
        (shape(BF, N, HALF, width), shape(BF, N, 48, 256)),
        arrived,
        down_share,
        scratch=[((HALF, lanes + width), BF)],
    )
    columns = jnp.stack([columns, shift(columns, "xh", 1, 2)])
    columns = jnp.stack([columns] + [shift(columns, "z", -k, 4) for k in (1, 2, 3)])

    share = to_all(sum_at(share, SPREAD).astype(BF), SPREAD)
    other_columns = shift(columns, "c", 1, 2)
    share, other_columns = lax.optimization_barrier((share, other_columns))
    other_share = shift(share, "c", 1, 2)
    units_out = (shape(F32, part, N * units),) * 2
    units_out = call(
        unpack_units, units_out, place, columns, other_columns, scalars=1
    )
    grad_w_gate, grad_w_up = [grad[None] for grad in units_out]
    narrow = [shape(F32, 1, count) for count in (part, k16, k16, part, part)]
    down, w_q, w_k, w_v, w_o, b_q, b_k, b_v, first, second = call(
        unpack_last,
        (
            shape(F32, units, width),
            shape(F32, part, width),
            shape(F32, part, kv),
            shape(F32, part, kv),
            shape(F32, part, width),
            *narrow,
        ),
        core,
        share,
        other_share,
        scalars=1,
    )
    weights = (first, w_q[None], b_q, w_k[None], b_k, w_v[None], b_v, w_o[None], second)
    return (hidden_out, grad_in) + weights + (grad_w_gate, grad_w_up, down[None])


def solution(mesh):
    split = Mesh(mesh.devices.reshape(SIZES), AXES)
    tokens = P(REPLICA, GROUP, None)
    vector = P(None, GROUP)
    matrix = P(None, GROUP, None)
    weights = (vector, matrix, vector, matrix, vector, matrix, vector, matrix, vector)
    return jax.shard_map(
        local,
        mesh=split,
        in_specs=(tokens, P(REPLICA, None)) + weights + (matrix,) * 3 + (tokens,),
        out_specs=(tokens, tokens) + weights + (matrix,) * 3,
        check_vma=False,
    )
```
